256 devices in a mesh: dp: 64 (over x, z, core), fsdp: 4 (over y).
Axes of the slice: x: 4, y: 4, z: 8, core: 2. Of those that a mesh axis runs over, the one named last changes fastest.
Arguments:
- query_reps: bfloat16 [4096, 4096], P('dp', 'fsdp'), may hold values from -2 to 2
- positive_reps: bfloat16 [4096, 4096], P('dp', 'fsdp'), may hold values from -8 to 8
- pool_reps: bfloat16 [8192, 4096], P('dp', 'fsdp'), may hold values from -8 to 8
- neg_owner: int32 [4096, 7], P('dp'), may hold values from 0 to 63, all different within a row; in each aligned block of 64 rows (0 to 63, 64 to 127, ...) at most 14 rows name the same one
- neg_row: int32 [4096, 7], P('dp'), may hold values from 0 to 127
- resid_in: bfloat16 [16384, 4096], P('dp', 'fsdp'), may hold values from -40 to 40
- attn_out: bfloat16 [16384, 2048], P('dp'), may hold values from -6 to 6
- out_weight: bfloat16 [2048, 4096], P(None, 'fsdp'), may hold values from -0.125 to 0.125
- norm_gain: float32 [4096], P('fsdp'), may hold values from 0.25 to 1.75
Outputs:
- resid_grad: bfloat16 [16384, 4096], P('dp', 'fsdp')
- attn_grad: bfloat16 [16384, 2048], P(('dp', 'fsdp'))
- weight_grad: bfloat16 [64, 2048, 4096], P('dp', None, 'fsdp')
- matching_reps_sensitivity: bfloat16 [4096, 4096], P('dp', 'fsdp')
- pool_grad: bfloat16 [8192, 4096], P('dp', 'fsdp')
The draws below stay inside these ranges and needn't reach their ends.
Inputs may be any that keep to these rules, and one draw needn't show every extreme that they name: `neg_owner`: the 7 negatives of one query lie with different dp indices; among the queries of one micro-batch at most 14 negatives lie with one dp index, and some dp index holds exactly 14 in some micro-batch.
All inputs are finite; a program needn't handle non-finite values.
Results may differ from the reference program's by a relative error of at most 0.015.
Values may be sent and summed in bfloat16 or wider, within the bound.
No kernel may reach another device: no remote copies, remote signals or barrier semaphores. Data moves between devices by JAX's collectives and lax.ppermute only.
A program may use at most 128 MiB of HBM per device.

```python
import math
import jax
import jax.numpy as jnp
import numpy as np
from jax import lax

D = 4096
HD = 2048
NEG = 7
QLEN = 16
Q_GRP = 64
CH_Q = 16
POOL_GRP = 128
CAP = 14
QUERIES = 4096
POOL = 8192
TOKENS = 16384
N_DP = 64


def spread_scales(key, count, span):
    return jnp.exp(jax.random.uniform(key, (count,), jnp.float32, -span, span))


def shape_rows(key, noise, base, row_span):
    key_col, key_row = jax.random.split(key, 2)
    column_scale = spread_scales(key_col, noise.shape[1], 1.15)
    row_scale = spread_scales(key_row, noise.shape[0], row_span)
    return base * row_scale[:, None] * column_scale[None, :] * noise


def noisy_values(key, count, width, base):
    key_noise, key_shape = jax.random.split(key)
    noise = jnp.clip(jax.random.normal(key_noise, (count, width), jnp.float32), -4.0, 4.0)
    values = shape_rows(key_shape, noise, base, 1.15)
    return values


def positive_values(key):
    return noisy_values(jax.random.fold_in(key, 12), QUERIES, D, 0.0625)


def draw_query_reps(key, part):
    key = jax.random.fold_in(key, 11)
    return noisy_values(key, QUERIES, D, 0.0156).astype(jnp.bfloat16)


def draw_positive_reps(key, part):
    return positive_values(key).astype(jnp.bfloat16)


def draw_pool_reps(key, part):
    key = jax.random.fold_in(key, 13)
    return noisy_values(key, POOL, D, 0.0625).astype(jnp.bfloat16)


def draw_resid_in(key, part):
    matched = positive_values(key).astype(jnp.bfloat16).astype(jnp.float32)
    key = jax.random.fold_in(key, 14)
    own_part = noisy_values(key, TOKENS, D, 0.5)
    token_rows = jnp.arange(TOKENS, dtype=jnp.int32)
    block_rows = CH_Q * QLEN
    owner_query = (token_rows // block_rows * Q_GRP + token_rows % block_rows // QLEN).astype(jnp.int32)
    along = jnp.take(matched, owner_query, axis=0)
    return jnp.clip(own_part + 6.0 * along, -40.0, 40.0).astype(jnp.bfloat16)


def plant(values, own_key, low, high):
    spot = [jax.random.randint(jax.random.fold_in(own_key, axis), (), 0, length) for axis, length in enumerate(values.shape)]
    main_axis = values.shape.index(max(values.shape))
    next_to = spot[:main_axis] + [(spot[main_axis] + 1) % values.shape[main_axis]] + spot[main_axis + 1:]
    return values.at[tuple(spot)].set(low).at[tuple(next_to)].set(high)


def steps_of(stream_key, extent, cuts, least, top_value):
    gain = 1.0
    for axis_at, blocks in cuts:
        draws = jax.random.uniform(jax.random.fold_in(jax.random.fold_in(stream_key, 6), axis_at), (blocks,), jnp.float32, least / len(cuts), top_value / len(cuts))
        gain = gain * jnp.repeat(jnp.exp(draws), extent[axis_at] // blocks).reshape((-1,) + (1,) * (len(extent) - 1 - axis_at))
    return gain


def shared_out(rng, own, number, rows, number_of, top, limit, skew):
    sequence = jax.random.permutation(rng, number_of)
    heavy_load, usual = portions_of(number_of, rows * top, limit, skew, True), portions_of(number_of, rows * top, limit, skew, False)
    places = jnp.arange(number_of)

    def named(sizes, rotation):
        used = int((sizes > 0).sum())
        fixed = max(1, used // 4)
        moved = fixed + (places - fixed + rotation * (used - fixed)) % max(1, number_of - fixed)
        return jnp.zeros((number_of,), jnp.int32).at[sequence[jnp.where(places < fixed, places, moved)]].set(jnp.asarray(sizes, jnp.int32))

    sizes = jnp.where(number % 4 == 0, named(heavy_load, number // 4), named(usual, number - number // 4 - 1))
    mixed = jax.random.permutation(jax.random.fold_in(own, 3), number_of)
    source_of, taker = mixed[0:number_of // 2 * 2:2], mixed[1:number_of // 2 * 2:2]
    margin = jnp.minimum(sizes[source_of] - 1, limit - sizes[taker]) // 2
    margin = jnp.where((source_of == sequence[0]) | (taker == sequence[0]) | (sizes[taker] == 0), 0, jnp.maximum(margin, 0))
    moved = jax.random.randint(jax.random.fold_in(own, 4), (number_of // 2,), 0, 1 << 20) % (margin + 1)
    sizes = sizes.at[source_of].add(-moved).at[taker].add(moved)
    items = jnp.searchsorted(jnp.cumsum(sizes), jnp.arange(rows * top), side="right").astype(jnp.int32)
    grid = items.reshape(top, rows).T
    grid = grid[jax.random.permutation(jax.random.fold_in(own, 1), rows)]
    rotation = jax.random.randint(jax.random.fold_in(own, 2), (rows, 1), 0, top)
    return jnp.take_along_axis(grid, (jnp.arange(top)[None, :] + rotation) % top, axis=1)


def portions_of(number_of, total, reach, lean, full):
    loads = [(1 << 20) // math.isqrt(rank ** lean) + 1 for rank in range(1, number_of + 1)]
    largest = reach if full else min(reach, max(-(-total // number_of), total * loads[0] // sum(loads)))
    least = 1 if total - largest >= number_of - 1 else 0
    counts, surplus = [largest] + [least] * (number_of - 1), total - largest - least * (number_of - 1)
    while surplus > 0:
        movable = [i for i in range(1, number_of) if counts[i] < largest] or [i for i in range(1, number_of) if counts[i] < reach]
        pool, remaining = sum([loads[i] for i in movable]), surplus
        for i in movable:
            addition = min(reach - counts[i], max(1, remaining * loads[i] // pool), surplus)
            counts[i] = counts[i] + addition
            surplus = surplus - addition
    return np.array(counts)


def normal_values(key, shape, spread, bound, cuts=(), held_as=jnp.bfloat16):
    drawn = jax.random.normal(key, shape, jnp.float32) * spread
    if len(cuts) > 0:
        drawn = steps_of(key, shape, cuts, -0.22, 0.18) * drawn
    return jnp.clip(drawn, min=-bound, max=bound).astype(held_as)


def setup_inputs(seed: int = 0) -> dict:
    splits = jax.random.split(jax.random.key(seed), 10)
    query_reps = draw_query_reps(jax.random.fold_in(splits[9], 71), 0)
    positive_reps = draw_positive_reps(jax.random.fold_in(splits[9], 71), 0)
    pool_reps = draw_pool_reps(jax.random.fold_in(splits[9], 71), 0)
    neg_owner_keys = jax.random.split(jax.random.fold_in(splits[3], 1), QUERIES // Q_GRP)
    neg_owner_turns = jax.random.permutation(jax.random.fold_in(splits[3], 3), QUERIES // Q_GRP)
    neg_owner = jax.vmap(lambda own, number: shared_out(jax.random.fold_in(splits[3], 2), own, number, Q_GRP, N_DP, NEG, CAP, 2))(neg_owner_keys, neg_owner_turns).reshape((QUERIES, NEG))
    neg_row = plant(jax.random.randint(splits[4], (QUERIES, NEG), 0, POOL_GRP), jax.random.fold_in(splits[4], 1), 0, POOL_GRP - 1).astype(jnp.int32)
    resid_in = draw_resid_in(jax.random.fold_in(splits[9], 71), 0)
    attn_out = normal_values(splits[6], (TOKENS, HD), 1.0, 6.0, ((0, 64),))
    out_weight = normal_values(splits[7], (HD, D), HD ** -0.5, 0.125, ((1, 4),))
    norm_gain = jnp.clip(1.0 + 0.15 * jax.random.normal(splits[8], (D,), jnp.float32), 0.25, 1.75)
    return {"query_reps": query_reps, "positive_reps": positive_reps, "pool_reps": pool_reps, "neg_owner": neg_owner, "neg_row": neg_row, "resid_in": resid_in, "attn_out": attn_out, "out_weight": out_weight, "norm_gain": norm_gain}


logit_sharpness_divisor = 0.05
objective_scale_factor = 32.0
rep_epsilon = 1e-06
norm_epsilon = 1e-05
exact_arithmetic_mode = lax.Precision.HIGHEST

def candidate_grads(query_b, positive_b, negatives_b):
    asker_wide_reps = query_b.astype(jnp.float32)
    matching_wide_reps = positive_b.astype(jnp.float32)
    distractor_wide_reps = negatives_b.astype(jnp.float32)
    asker_reciprocal_length = lax.rsqrt(lax.optimization_barrier(jnp.sum(asker_wide_reps * asker_wide_reps, axis=1)) + rep_epsilon)
    matching_reciprocal_length = lax.rsqrt(lax.optimization_barrier(jnp.sum(matching_wide_reps * matching_wide_reps, axis=1)) + rep_epsilon)
    distractor_reciprocal_length = lax.rsqrt(lax.optimization_barrier(jnp.sum(distractor_wide_reps * distractor_wide_reps, axis=2)) + rep_epsilon)
    sibling_cosine_matrix = jnp.dot(query_b, positive_b.T, preferred_element_type=jnp.float32)
    distractor_cosine_matrix = jnp.einsum('qd,qkd->qk', asker_wide_reps, distractor_wide_reps, precision=exact_arithmetic_mode)
    sibling_logit_matrix = sibling_cosine_matrix * asker_reciprocal_length[:, None] * matching_reciprocal_length[None, :] / logit_sharpness_divisor
    distractor_logit_matrix = distractor_cosine_matrix * asker_reciprocal_length[:, None] * distractor_reciprocal_length / logit_sharpness_divisor
    exp_inbatch = jnp.exp(sibling_logit_matrix)
    exp_negative = jnp.exp(distractor_logit_matrix)
    total = lax.optimization_barrier(jnp.sum(exp_inbatch, axis=1)) + lax.optimization_barrier(jnp.sum(exp_negative, axis=1))
    sibling_pair_factor = exp_inbatch / total[:, None] - jnp.eye(Q_GRP, dtype=jnp.float32)
    distractor_pair_factor = exp_negative / total[:, None]
    self_dot = objective_scale_factor * (lax.optimization_barrier(jnp.sum(sibling_pair_factor * sibling_logit_matrix, axis=1)) + lax.optimization_barrier(jnp.sum(distractor_pair_factor * distractor_logit_matrix, axis=1)))
    update_step_vector = objective_scale_factor / logit_sharpness_divisor * (jnp.dot(sibling_pair_factor * matching_reciprocal_length[None, :], matching_wide_reps, precision=exact_arithmetic_mode) + jnp.einsum('ak,akr->ar', distractor_pair_factor * distractor_reciprocal_length, distractor_wide_reps, precision=exact_arithmetic_mode))
    query_grad = asker_reciprocal_length[:, None] * update_step_vector - (asker_reciprocal_length * asker_reciprocal_length * self_dot)[:, None] * asker_wide_reps
    matching_reps_sensitivity = objective_scale_factor / logit_sharpness_divisor * matching_reciprocal_length[:, None] * jnp.dot((sibling_pair_factor * asker_reciprocal_length[:, None]).T, asker_wide_reps, precision=exact_arithmetic_mode)
    matching_reps_sensitivity = matching_reps_sensitivity - (matching_reciprocal_length * matching_reciprocal_length * objective_scale_factor * lax.optimization_barrier(jnp.sum(sibling_pair_factor * sibling_logit_matrix, axis=0)))[:, None] * matching_wide_reps
    asker_output_matrix = objective_scale_factor / logit_sharpness_divisor * distractor_pair_factor * asker_reciprocal_length[:, None] * distractor_reciprocal_length
    weight_negative = objective_scale_factor * distractor_pair_factor * distractor_logit_matrix * distractor_reciprocal_length * distractor_reciprocal_length
    negative_grad = asker_output_matrix[:, :, None] * asker_wide_reps[:, None, :] - weight_negative[:, :, None] * distractor_wide_reps
    return (query_grad, matching_reps_sensitivity, negative_grad)

def reference(query_reps, positive_reps, pool_reps, neg_owner, neg_row, resid_in, attn_out, out_weight, norm_gain):
    pool_index = (neg_owner * POOL_GRP + neg_row).astype(jnp.int32).reshape(N_DP, Q_GRP * NEG)
    queries = query_reps.reshape(N_DP, Q_GRP, D)
    positives = positive_reps.reshape(N_DP, Q_GRP, D)

    def group_step(pool_total, pieces):
        query_b, positive_b, pool_rows = pieces
        negatives_b = jnp.take(pool_reps, pool_rows, axis=0).reshape(Q_GRP, NEG, D)
        query_grad, matching_reps_sensitivity, negative_grad = candidate_grads(query_b, positive_b, negatives_b)
        pool_total = pool_total.at[pool_rows].add(negative_grad.reshape(Q_GRP * NEG, D))
        return (pool_total, (query_grad[:CH_Q], matching_reps_sensitivity.astype(jnp.bfloat16)))
    pool_total, outputs = lax.scan(group_step, jnp.zeros((POOL, D), jnp.float32), (queries, positives, pool_index))
    stretch_grads, positive_grads = outputs
    token_count = CH_Q * QLEN

    def stretch_step(pieces):
        resid_b, attn_b, query_grad = pieces
        hidden = resid_b.astype(jnp.float32) + jnp.dot(attn_b, out_weight, preferred_element_type=jnp.float32)
        inv_rms = lax.rsqrt(lax.optimization_barrier(jnp.mean(hidden * hidden, axis=1)) + norm_epsilon)
        pooled_grad = jnp.repeat(query_grad / QLEN, QLEN, axis=0)
        inner_sum = lax.optimization_barrier(jnp.sum(hidden * norm_gain[None, :] * pooled_grad, axis=1))
        cubed = inv_rms * inv_rms * inv_rms
        hidden_grad = inv_rms[:, None] * norm_gain[None, :] * pooled_grad - hidden * (cubed * inner_sum / D)[:, None]
        hidden_grad = hidden_grad.astype(jnp.bfloat16)
        attn_grad = jnp.dot(hidden_grad, out_weight.T, preferred_element_type=jnp.float32).astype(jnp.bfloat16)
        weight_grad = jnp.dot(attn_b.T, hidden_grad, preferred_element_type=jnp.float32).astype(jnp.bfloat16)
        return (hidden_grad, attn_grad, weight_grad)
    resid_grad, attn_grad, weight_grad = lax.map(stretch_step, (resid_in.reshape(N_DP, token_count, D), attn_out.reshape(N_DP, token_count, HD), stretch_grads))
    return (resid_grad.reshape(TOKENS, D), attn_grad.reshape(TOKENS, HD), weight_grad, positive_grads.reshape(QUERIES, D), pool_total.astype(jnp.bfloat16))
```

```python
import jax
import jax.numpy as jnp
from jax import lax
from jax.sharding import PartitionSpec as P

D = 4096
NEG = 7
QLEN = 16
Q_GRP = 64
CH_Q = 16
POOL_GRP = 128
SLOTS = 16
N_FS = 4


inv_temp = 1.0 / 0.05
loss_scale = 32.0
rep_epsilon = 1e-06
norm_epsilon = 1e-05
F32 = jnp.float32
BF16 = jnp.bfloat16


def dot(a, b, ca, cb):
    return lax.dot_general(a, b, (((ca,), (cb,)), ((), ())), preferred_element_type=F32)


def dot_exact(a, b, ca, cb):
    return lax.dot_general(
        a, b, (((ca,), (cb,)), ((), ())), precision=lax.Precision.HIGHEST, preferred_element_type=F32
    )


def split(a):
    hi = a.astype(BF16)
    return hi, (a - hi.astype(F32)).astype(BF16)


def shifted(value, step):
    return lax.ppermute(value, "fsdp", [(i, (i + step) % N_FS) for i in range(N_FS)])


def feature_total(rows):
    return rows + shifted(rows, 1) + shifted(rows, 3) + shifted(rows, 2)


def feature_scatter(rows):
    own = rows.shape[0] // N_FS
    me = lax.axis_index("fsdp")
    total = lax.dynamic_slice(rows, (me * own, 0), (own, rows.shape[1]))
    for step in (1, 3, 2):
        there = lax.rem(me + step, N_FS)
        total += shifted(lax.dynamic_slice(rows, (there * own, 0), (own, rows.shape[1])), step)
    return total


def per_device(q, pos, pool, neg_owner, neg_row, resid_in, attn_out, out_weight, norm_gain):
    owners = lax.axis_size("dp")
    cols = q.shape[1]
    requests = Q_GRP * NEG
    tokens = resid_in.shape[0]
    slot_rows = owners * SLOTS

    q_all = lax.all_gather(q, "dp", tiled=True)

    owner_t = neg_owner.T
    row_t = neg_row.T
    owner_hot = (owner_t[:, :, None] == jnp.arange(owners)[None, None, :]).astype(BF16)
    owner_hot = owner_hot.reshape(requests, owners)
    order = jnp.arange(requests)
    earlier = (order[:, None] > order[None, :]).astype(BF16)
    before = dot(earlier, owner_hot, 1, 0)
    position = jnp.sum(before * owner_hot.astype(F32), axis=1).astype(jnp.int32)
    place_hot = (position[:, None] == jnp.arange(SLOTS)[None, :]).astype(BF16)
    row_mark = (row_t + 1).astype(BF16).reshape(requests, 1)
    query_mark = jnp.broadcast_to((jnp.arange(Q_GRP) + 1).astype(BF16)[None, :], (NEG, Q_GRP))
    query_mark = query_mark.reshape(requests, 1)
    table = dot(
        owner_hot, jnp.concatenate([place_hot * row_mark, place_hot * query_mark], axis=1), 0, 0
    ).astype(jnp.int32)
    code = table[:, :SLOTS] * 128 + table[:, SLOTS:]
    wanted = lax.all_to_all(code, "dp", split_axis=0, concat_axis=0, tiled=True)
    wanted_row = wanted // 128 - 1
    wanted_query = wanted % 128 - 1
    row_hot = (wanted_row.reshape(slot_rows)[:, None] == jnp.arange(POOL_GRP)[None, :]).astype(BF16)
    fetched = dot(row_hot, pool, 1, 0).astype(BF16).reshape(owners, SLOTS, cols)
    replies = lax.all_to_all(fetched, "dp", split_axis=0, concat_axis=0, tiled=True)

    fetched, q, pos, resid_in, attn_out = lax.optimization_barrier(
        (fetched, q, pos, resid_in, attn_out)
    )
    q_wide = q.astype(F32)
    pos_wide = pos.astype(F32)
    attn_turned = attn_out.T
    hidden = resid_in.astype(F32) + dot(attn_out, out_weight, 1, 0)
    hid_hi, hid_lo = split(hidden)
    scaled_hi, scaled_lo = split(hidden * norm_gain[None, :])
    both = jnp.concatenate([pos, q], axis=0)
    scaled_dots = dot(scaled_hi, both, 1, 1) + dot(scaled_lo, both, 1, 1)
    lane = jnp.arange(2 * Q_GRP)
    scaled_dots = jnp.where(
        lane[None, :] == 2 * Q_GRP - 1, jnp.sum(hidden * hidden, axis=1)[:, None], scaled_dots
    )
    p_row = jnp.concatenate([jnp.sum(pos_wide * pos_wide, axis=1), jnp.zeros((Q_GRP,), F32)])
    early = feature_total(
        jnp.concatenate(
            [scaled_dots, dot(q, both, 1, 1), jnp.broadcast_to(p_row[None, :], (8, 2 * Q_GRP))],
            axis=0,
        )
    )
    hidden_back = feature_scatter(dot(hid_hi, out_weight, 1, 1) + dot(hid_lo, out_weight, 1, 1))
    eye = jnp.eye(Q_GRP, dtype=F32)
    q_sq = jnp.sum(early[tokens : tokens + Q_GRP, Q_GRP:] * eye, axis=1)
    p_sq = early[tokens + Q_GRP, :Q_GRP]
    h_sq = early[:tokens, 2 * Q_GRP - 1]
    inv_q = lax.rsqrt(q_sq + rep_epsilon)
    inv_p = lax.rsqrt(p_sq + rep_epsilon)
    inv_rms = lax.rsqrt(h_sq / D + norm_epsilon)
    s_in = early[tokens : tokens + Q_GRP, :Q_GRP] * inv_q[:, None] * inv_p[None, :] * inv_temp
    exp_in = jnp.exp(s_in)
    sum_in = jnp.sum(exp_in, axis=1)
    token_query = jnp.arange(tokens) // QLEN
    scaled_pos = early[:tokens, :Q_GRP]
    scaled_q = jnp.sum(
        jnp.where(
            token_query[:, None] == jnp.arange(CH_Q)[None, :],
            early[:tokens, Q_GRP : Q_GRP + CH_Q],
            0.0,
        ),
        axis=1,
    )
    replies, sum_in, scaled_q, attn_turned, hidden_back, inv_rms = lax.optimization_barrier(
        (replies, sum_in, scaled_q, attn_turned, hidden_back, inv_rms)
    )

    slot = owner_t.reshape(requests) * SLOTS + position
    slot_hot = (slot[:, None] == jnp.arange(slot_rows)[None, :]).astype(BF16)
    negs = dot(slot_hot, replies.reshape(slot_rows, cols), 1, 0).astype(BF16)
    negs = negs.reshape(NEG, Q_GRP, cols)
    negs_wide = negs.astype(F32)
    n_cos = jnp.sum(negs_wide * q_wide[None], axis=2)
    n_sq = jnp.sum(negs_wide * negs_wide, axis=2)
    first_negs = negs[:, :CH_Q].reshape(NEG * CH_Q, cols)
    scaled_negs = dot(scaled_hi, first_negs, 1, 1) + dot(scaled_lo, first_negs, 1, 1)
    scaled_negs = jnp.sum(
        jnp.where(
            token_query[:, None, None] == jnp.arange(CH_Q)[None, None, :],
            scaled_negs.reshape(tokens, NEG, CH_Q),
            0.0,
        ),
        axis=2,
    )
    late = feature_total(
        jnp.concatenate(
            [
                jnp.concatenate([n_cos, jnp.zeros((1, Q_GRP), F32)], axis=0),
                jnp.concatenate([n_sq, jnp.zeros((1, Q_GRP), F32)], axis=0),
                scaled_negs.T.reshape(NEG * tokens // Q_GRP, Q_GRP),
            ],
            axis=0,
        )
    )
    n_cos = late[:NEG]
    n_sq = late[NEG + 1 : 2 * NEG + 1]
    scaled_negs = late[2 * NEG + 2 :].reshape(NEG, tokens)
    inv_n = lax.rsqrt(n_sq + rep_epsilon)
    s_neg = n_cos * inv_q[None, :] * inv_n * inv_temp
    exp_neg = jnp.exp(s_neg)
    denominator = sum_in + jnp.sum(exp_neg, axis=0)
    coef_in = exp_in / denominator[:, None] - eye
    coef_neg = exp_neg / denominator[None, :]

    w_q = loss_scale * inv_temp * coef_neg * inv_q[None, :] * inv_n
    w_n = loss_scale * coef_neg * s_neg * inv_n * inv_n
    place = place_hot.astype(F32)
    sent = dot_exact(
        owner_hot.astype(F32),
        jnp.concatenate(
            [place * w_q.reshape(requests, 1), place * w_n.reshape(requests, 1)], axis=1
        ),
        0,
        0,
    )
    got = lax.all_to_all(sent, "dp", split_axis=0, concat_axis=0, tiled=True)

    self_dot = loss_scale * (jnp.sum(coef_in * s_in, axis=1) + jnp.sum(coef_neg * s_neg, axis=0))
    pos_part = (coef_in * inv_p[None, :])[:CH_Q]
    neg_part = (coef_neg * inv_n)[:, :CH_Q]
    direction = dot_exact(pos_part, pos_wide, 1, 0) + jnp.sum(
        neg_part[:, :, None] * negs_wide[:, :CH_Q], axis=0
    )
    inv_c = inv_q[:CH_Q]
    scale_dir = loss_scale * inv_temp * inv_c * (1.0 / QLEN)
    scale_own = inv_c * inv_c * self_dot[:CH_Q] * (1.0 / QLEN)
    pooled = scale_dir[:, None] * direction - scale_own[:, None] * q_wide[:CH_Q]
    gained = pooled * norm_gain[None, :]
    inner = jnp.repeat(scale_dir, QLEN) * (
        jnp.sum(jnp.repeat(pos_part, QLEN, axis=0) * scaled_pos, axis=1)
        + jnp.sum(jnp.repeat(neg_part, QLEN, axis=1) * scaled_negs, axis=0)
    ) - jnp.repeat(scale_own, QLEN) * scaled_q
    hidden_c = hidden.reshape(CH_Q, QLEN, cols)
    shrink = inv_rms * inv_rms * inv_rms * inner * (1.0 / D)
    g_hi, g_lo = split(gained)
    gained_back = dot(jnp.concatenate([g_hi, g_lo], axis=0), out_weight, 1, 1)
    gained_back = feature_scatter(gained_back[:CH_Q] + gained_back[CH_Q:])
    resid_grad = (
        inv_rms.reshape(CH_Q, QLEN, 1) * gained[:, None, :]
        - hidden_c * shrink.reshape(CH_Q, QLEN, 1)
    ).reshape(tokens, cols).astype(BF16)
    own = tokens // N_FS
    first = lax.axis_index("fsdp") * own
    own_rms = lax.dynamic_slice(inv_rms, (first,), (own,))
    own_shrink = lax.dynamic_slice(shrink, (first,), (own,))
    gained_rows = jnp.broadcast_to(
        gained_back[:, None, :], (CH_Q // N_FS, QLEN, gained_back.shape[1])
    ).reshape(own, gained_back.shape[1])
    attn_grad = (own_rms[:, None] * gained_rows - own_shrink[:, None] * hidden_back).astype(BF16)
    weight_grad = dot(attn_turned, resid_grad, 1, 0).astype(BF16)[None]

    back = dot_exact(coef_in * inv_q[:, None], q_wide, 0, 0)
    pos_grad = (loss_scale * inv_temp) * inv_p[:, None] * back - (
        inv_p * inv_p * loss_scale * jnp.sum(coef_in * s_in, axis=0)
    )[:, None] * pos_wide

    query_hot = (wanted_query[:, :, None] == jnp.arange(Q_GRP)[None, None, :]).astype(BF16)
    askers = lax.dot_general(
        query_hot,
        q_all.reshape(owners, Q_GRP, cols),
        (((2,), (1,)), ((0,), (0,))),
        preferred_element_type=F32,
    ).astype(BF16).reshape(slot_rows, cols)
    row_wide = row_hot.astype(F32)
    weighted = row_wide * got[:, :SLOTS].reshape(slot_rows, 1)
    row_hi, row_lo = split(weighted)
    row_weight = jnp.sum(row_wide * got[:, SLOTS:].reshape(slot_rows, 1), axis=0)
    pool_grad = (
        dot(row_hi, askers, 0, 0)
        + dot(row_lo, askers, 0, 0)
        - row_weight[:, None] * pool.astype(F32)
    )
    return (
        resid_grad,
        attn_grad,
        weight_grad,
        pos_grad.astype(BF16),
        pool_grad.astype(BF16),
    )


def solution(mesh):
    placed = (
        P("dp", "fsdp"),
        P("dp", "fsdp"),
        P("dp", "fsdp"),
        P("dp", None),
        P("dp", None),
        P("dp", "fsdp"),
        P("dp", None),
        P(None, "fsdp"),
        P("fsdp"),
    )
    return jax.shard_map(
        per_device,
        mesh=mesh,
        in_specs=placed,
        out_specs=(
            P("dp", "fsdp"),
            P(("dp", "fsdp"), None),
            P("dp", None, "fsdp"),
            P("dp", "fsdp"),
            P("dp", "fsdp"),
        ),
        check_vma=False,
    )
```

```python
import jax
import jax.numpy as jnp
from jax import lax
from jax.experimental import pallas as pl
from jax.experimental.pallas import tpu as pltpu
from jax.sharding import PartitionSpec as P

D = 4096
NEG = 7
QLEN = 16
Q_GRP = 64
CH_Q = 16
POOL_GRP = 128
SLOTS = 14
WIDE = 16
SUB = 8
LANES = 128
VMEM_LIMIT = 24 * 1024 * 1024
N_FS = 4


inv_temp = 1.0 / 0.05
loss_scale = 32.0
rep_epsilon = 1e-06
norm_epsilon = 1e-05
F32 = jnp.float32
BF16 = jnp.bfloat16


def dot(a, b, ca, cb):
    return lax.dot_general(a, b, (((ca,), (cb,)), ((), ())), preferred_element_type=F32)


def dot_exact(a, b, ca, cb):
    return lax.dot_general(
        a, b, (((ca,), (cb,)), ((), ())), precision=lax.Precision.HIGHEST, preferred_element_type=F32
    )


def split(a):
    hi = a.astype(BF16)
    return hi, (a - hi.astype(F32)).astype(BF16)


def shifted(value, step):
    return lax.ppermute(value, "fsdp", [(i, (i + step) % N_FS) for i in range(N_FS)])


def swapped(value, mask):
    return lax.ppermute(value, "fsdp", [(i, i ^ mask) for i in range(N_FS)])


def feature_total(rows):
    return rows + shifted(rows, 1) + shifted(rows, 3) + shifted(rows, 2)


def feature_scatter_small(rows):
    own = rows.shape[0] // N_FS
    me = lax.axis_index("fsdp")
    half = me // 2
    mine = lax.dynamic_slice(rows, (half * 2 * own, 0), (2 * own, rows.shape[1]))
    other = lax.dynamic_slice(rows, ((1 - half) * 2 * own, 0), (2 * own, rows.shape[1]))
    mine = mine + swapped(other, 3)
    side = me % 2
    kept = lax.dynamic_slice(mine, (side * own, 0), (own, rows.shape[1]))
    given = lax.dynamic_slice(mine, ((1 - side) * own, 0), (own, rows.shape[1]))
    return kept + swapped(given, 1)


def feature_scatter(rows):
    own = rows.shape[0] // N_FS
    me = lax.axis_index("fsdp")
    total = lax.dynamic_slice(rows, (me * own, 0), (own, rows.shape[1]))
    for step in (1, 3, 2):
        there = lax.rem(me + step, N_FS)
        total += shifted(lax.dynamic_slice(rows, (there * own, 0), (own, rows.shape[1])), step)
    return total


def eye_of(rows, cols):
    down = lax.broadcasted_iota(jnp.int32, (rows, cols), 0)
    return (down == lax.broadcasted_iota(jnp.int32, (rows, cols), 1)).astype(F32)


def to_column(row):
    size = row.shape[1]
    return jnp.sum(eye_of(size, size) * row, axis=1, keepdims=True)


def tiled(values, period, times):
    width = period * times
    down = lax.broadcasted_iota(jnp.int32, (period, width), 0)
    along = lax.broadcasted_iota(jnp.int32, (period, width), 1)
    return dot_exact(values, (along % period == down).astype(F32), 1, 0)


def flat_row(values, times):
    rows, period = values.shape
    wide = tiled(values, period, times)
    down = lax.broadcasted_iota(jnp.int32, wide.shape, 0)
    along = lax.broadcasted_iota(jnp.int32, wide.shape, 1)
    return jnp.sum(jnp.where(along // period == down, wide, 0.0), axis=0, keepdims=True)


def request_kernel(name_ref, code_ref, slot_ref, turned_ref, place_ref):
    name = flat_row(name_ref[...].astype(F32), NEG).astype(jnp.int32)
    owner = lax.shift_right_logical(name, 7).astype(F32)
    row = jnp.bitwise_and(name, 127).astype(F32)
    requests = owner.shape[1]
    peers = turned_ref.shape[0]
    along = lax.broadcasted_iota(jnp.int32, (1, requests), 1)
    down = lax.broadcasted_iota(jnp.int32, (peers, requests), 0)
    hot = jnp.where(down == owner.astype(jnp.int32), 1.0, 0.0)
    turned = hot.astype(BF16)
    earlier = lax.broadcasted_iota(jnp.int32, (requests, requests), 0) < along
    before = dot(turned, jnp.where(earlier, 1.0, 0.0).astype(BF16), 1, 0)
    position = jnp.sum(hot * before, axis=0, keepdims=True)
    down = lax.broadcasted_iota(jnp.int32, (WIDE, requests), 0)
    place = jnp.where(down == position.astype(jnp.int32), 1.0, 0.0)
    query = (along % Q_GRP + 1).astype(F32)
    marks = jnp.concatenate([place * row, place * query], axis=0).astype(BF16)
    table = dot(turned, marks, 1, 1).astype(jnp.int32)
    code_ref[...] = table[:, :WIDE] * 128 + table[:, WIDE:]
    slot_ref[...] = (owner * SLOTS + position).astype(jnp.int32)
    turned_ref[...] = turned
    place_ref[...] = place.astype(BF16)


def request_tables(name, owners):
    requests = name.shape[0] * name.shape[1]
    vmem = pl.BlockSpec(memory_space=pltpu.VMEM)
    return pl.pallas_call(
        request_kernel,
        out_shape=(
            jax.ShapeDtypeStruct((owners, WIDE), jnp.int32),
            jax.ShapeDtypeStruct((1, requests), jnp.int32),
            jax.ShapeDtypeStruct((owners, requests), BF16),
            jax.ShapeDtypeStruct((WIDE, requests), BF16),
        ),
        in_specs=[vmem],
        out_specs=(vmem,) * 4,
        compiler_params=pltpu.CompilerParams(vmem_limit_bytes=VMEM_LIMIT),
        cost_estimate=pl.CostEstimate(flops=30000000, bytes_accessed=100000, transcendentals=0),
    )(name)


def fetch_kernel(code_ref, pool_ref, out_ref):
    @pl.loop(0, out_ref.shape[0])
    def _(peer):
        for place in range(SLOTS):
            out_ref[peer, place] = pool_ref[lax.shift_right_logical(code_ref[peer, place], 7)]


def fetch_rows(code, pool_tiles):
    peers = code.shape[0]
    return pl.pallas_call(
        fetch_kernel,
        out_shape=jax.ShapeDtypeStruct((peers, SLOTS, SUB, LANES), BF16),
        in_specs=[
            pl.BlockSpec(memory_space=pltpu.SMEM),
            pl.BlockSpec(memory_space=pltpu.VMEM),
        ],
        out_specs=pl.BlockSpec(memory_space=pltpu.VMEM),
        compiler_params=pltpu.CompilerParams(vmem_limit_bytes=VMEM_LIMIT),
        cost_estimate=pl.CostEstimate(flops=0, bytes_accessed=2 * 1835008, transcendentals=0),
    )(code, pool_tiles)


def row_sums_kernel(slot_ref, reply_ref, q_ref, sums_ref, first_ref, cos_ref, sq_ref):
    last = reply_ref.shape[0] - 1

    def one(query, keep):
        asked = q_ref[query].astype(F32)
        for k in range(NEG):
            row = reply_ref[jnp.clip(slot_ref[0, k * Q_GRP + query], 0, last)]
            if keep:
                first_ref[k * CH_Q + query] = row
            wide = row.astype(F32)
            at = pl.ds(k * Q_GRP + query, 1)
            cos_ref[at, :] = jnp.sum(wide * asked, axis=0, keepdims=True)
            sq_ref[at, :] = jnp.sum(wide * wide, axis=0, keepdims=True)

    pl.loop(0, CH_Q)(lambda query: one(query, True))
    pl.loop(CH_Q, Q_GRP)(lambda query: one(query, False))

    line = lax.broadcasted_iota(jnp.int32, (SUB, LANES), 0)
    for part, ref in ((0, cos_ref), (1, sq_ref)):
        total = jnp.zeros((SUB, Q_GRP), F32)
        for k in range(NEG):
            total += dot_exact((line == k).astype(F32), ref[k * Q_GRP : (k + 1) * Q_GRP, :], 1, 1)
        sums_ref[part * SUB : (part + 1) * SUB, :] = total


def row_sums(slot, replies, q_tiles):
    return pl.pallas_call(
        row_sums_kernel,
        out_shape=(
            jax.ShapeDtypeStruct((2 * SUB, Q_GRP), F32),
            jax.ShapeDtypeStruct((NEG * CH_Q, SUB, LANES), BF16),
        ),
        in_specs=[
            pl.BlockSpec(memory_space=pltpu.SMEM),
            pl.BlockSpec(memory_space=pltpu.VMEM),
            pl.BlockSpec(memory_space=pltpu.VMEM),
        ],
        out_specs=(
            pl.BlockSpec(memory_space=pltpu.VMEM),
            pl.BlockSpec(memory_space=pltpu.VMEM),
        ),
        scratch_shapes=[
            pltpu.VMEM((NEG * Q_GRP, LANES), F32),
            pltpu.VMEM((NEG * Q_GRP, LANES), F32),
        ],
        compiler_params=pltpu.CompilerParams(vmem_limit_bytes=VMEM_LIMIT),
        cost_estimate=pl.CostEstimate(flops=2000000, bytes_accessed=2200000, transcendentals=0),
    )(slot, replies, q_tiles)


def soft_kernel(
    late_ref, sum_ref, inv_q_ref, owner_ref, place_ref, sent_ref, coef_ref, logit_ref, inv_n_ref, den_ref
):
    late = late_ref[...]
    inv_q = inv_q_ref[...]
    inv_n = lax.rsqrt(late[:, Q_GRP : 2 * Q_GRP] + rep_epsilon)
    logit = late[:, :Q_GRP] * inv_q * inv_n * inv_temp
    used = lax.broadcasted_iota(jnp.int32, logit.shape, 0) < NEG
    raised = jnp.where(used, jnp.exp(logit), 0.0)
    total = sum_ref[...] + jnp.sum(raised, axis=0, keepdims=True)
    coef = raised / total
    coef_ref[...] = coef
    logit_ref[...] = logit
    inv_n_ref[...] = inv_n
    den_ref[...] = total
    w_q = flat_row(loss_scale * inv_temp * coef * inv_q * inv_n, NEG)
    w_n = flat_row(loss_scale * coef * logit * inv_n * inv_n, NEG)
    owner = owner_ref[...].astype(F32)
    parts = split(owner * w_q) + split(owner * w_n)
    placed = dot(jnp.concatenate(parts, axis=0), place_ref[...], 1, 1)
    peers = owner.shape[0]
    sent_ref[:, :WIDE] = placed[:peers] + placed[peers : 2 * peers]
    sent_ref[:, WIDE:] = placed[2 * peers : 3 * peers] + placed[3 * peers :]


def soft(late, sum_in, inv_q, owner_turned, place_hot):
    small = jax.ShapeDtypeStruct((SUB, Q_GRP), F32)
    vmem = pl.BlockSpec(memory_space=pltpu.VMEM)
    return pl.pallas_call(
        soft_kernel,
        out_shape=(
            jax.ShapeDtypeStruct((owner_turned.shape[0], 2 * WIDE), F32),
            small,
            small,
            small,
            jax.ShapeDtypeStruct((1, Q_GRP), F32),
        ),
        in_specs=[vmem] * 5,
        out_specs=(vmem,) * 5,
        compiler_params=pltpu.CompilerParams(vmem_limit_bytes=VMEM_LIMIT),
        cost_estimate=pl.CostEstimate(flops=8000000, bytes_accessed=100000, transcendentals=512),
    )(late, sum_in, inv_q, owner_turned, place_hot)


def grads_kernel(
    late_ref, coef_ref, logit_ref, inv_n_ref, den_ref, exp_ref, s_ref, inv_q_ref, inv_p_ref,
    rms_ref, scaled_pos_ref, scaled_q_ref, gain_ref, q_ref, pos_ref, negs_ref,
    gained_ref, halves_ref, shrink_ref, pos_grad_ref,
):
    eye = eye_of(Q_GRP, Q_GRP)
    inv_q_row = inv_q_ref[...]
    inv_p_row = inv_p_ref[...]
    inv_q = to_column(inv_q_row)
    coef_neg = coef_ref[...]
    coef_in = exp_ref[...] / to_column(den_ref[...]) - eye
    product = coef_in * s_ref[...]
    neg_dot = jnp.sum(coef_neg * logit_ref[...], axis=0, keepdims=True)
    self_dot = loss_scale * (jnp.sum(product, axis=1, keepdims=True) + to_column(neg_dot))
    scale_dir = loss_scale * inv_temp / QLEN * inv_q
    scale_own = inv_q * inv_q * self_dot * (1.0 / QLEN)
    of_pos = (coef_in * inv_p_row * scale_dir)[:CH_Q]
    neg_part = (coef_neg * inv_n_ref[...] * (loss_scale * inv_temp / QLEN) * inv_q_row)[:, :CH_Q]
    neg_row = flat_row(neg_part, NEG)
    down = lax.broadcasted_iota(jnp.int32, (CH_Q, NEG * CH_Q), 0)
    along = lax.broadcasted_iota(jnp.int32, (CH_Q, NEG * CH_Q), 1)
    of_neg = jnp.where(along % CH_Q == down, neg_row, 0.0)
    of_own = -eye[:CH_Q, :CH_Q] * scale_own[:CH_Q]
    both = (
        dot(jnp.concatenate(split(of_pos), axis=0), pos_ref[...], 1, 0)
        + dot(jnp.concatenate(split(of_neg), axis=0), negs_ref[...], 1, 0)
        + dot(jnp.concatenate(split(of_own), axis=0), q_ref[:CH_Q, :], 1, 0)
    )
    gained = (both[:CH_Q] + both[CH_Q:]) * gain_ref[...]
    gained_ref[...] = gained
    high, low = split(gained)
    halves_ref[:CH_Q, :] = high
    halves_ref[CH_Q:, :] = low
    tokens = CH_Q * QLEN
    down = lax.broadcasted_iota(jnp.int32, (CH_Q, tokens), 0)
    mine = lax.broadcasted_iota(jnp.int32, (CH_Q, tokens), 1) // QLEN == down
    inner = dot_exact(of_pos, scaled_pos_ref[...], 1, 0) - scale_own[:CH_Q] * scaled_q_ref[...]
    inner = jnp.sum(jnp.where(mine, inner, 0.0), axis=0, keepdims=True)
    spread = dot_exact(neg_part, mine.astype(F32), 1, 0)
    inner += jnp.sum(spread * late_ref[:, 2 * Q_GRP :], axis=0, keepdims=True)
    rms = rms_ref[...]
    shrink_ref[...] = rms * rms * rms * inner * (1.0 / D)
    back = coef_in * inv_q * (inv_p_row * (loss_scale * inv_temp))
    turned = dot(jnp.concatenate(split(back), axis=1), q_ref[...], 0, 0)
    less = to_column(inv_p_row * inv_p_row * loss_scale * jnp.sum(product, axis=0, keepdims=True))
    pos_grad_ref[...] = (
        turned[:Q_GRP] + turned[Q_GRP:] - less * pos_ref[...].astype(F32)
    ).astype(BF16)


def grads(*operands):
    vmem = pl.BlockSpec(memory_space=pltpu.VMEM)
    cols = operands[-1].shape[1]
    return pl.pallas_call(
        grads_kernel,
        out_shape=(
            jax.ShapeDtypeStruct((CH_Q, cols), F32),
            jax.ShapeDtypeStruct((2 * CH_Q, cols), BF16),
            jax.ShapeDtypeStruct((1, CH_Q * QLEN), F32),
            jax.ShapeDtypeStruct((Q_GRP, cols), BF16),
        ),
        in_specs=[vmem] * len(operands),
        out_specs=(vmem,) * 4,
        compiler_params=pltpu.CompilerParams(vmem_limit_bytes=VMEM_LIMIT),
        cost_estimate=pl.CostEstimate(flops=40000000, bytes_accessed=1000000, transcendentals=0),
    )(*operands)


def weight_kernel(
    hidden_ref, gained_ref, rms_ref, shrink_ref, attn_ref, resid_ref, out_ref, held_ref, tile_ref, sems
):
    rms = to_column(rms_ref[...])
    shrink = to_column(shrink_ref[...])
    for c in range(CH_Q):
        at = slice(c * QLEN, (c + 1) * QLEN)
        held_ref[at, :] = (
            rms[at] * gained_ref[c : c + 1, :] - shrink[at] * hidden_ref[at, :]
        ).astype(BF16)
    blocks, block = tile_ref.shape[0], tile_ref.shape[1]
    copies = [pltpu.make_async_copy(held_ref, resid_ref, sems.at[blocks])]
    copies[0].start()
    for b in range(blocks):
        at = slice(b * block, (b + 1) * block)
        tile_ref[b] = dot(attn_ref[at, :], held_ref[...], 1, 0).astype(BF16)
        copy = pltpu.make_async_copy(tile_ref.at[b], out_ref.at[pl.ds(b * block, block)], sems.at[b])
        copy.start()
        copies.append(copy)
    for copy in copies:
        copy.wait()


def weight_grads(hidden, gained, rms, shrink, attn_turned):
    tokens, cols = hidden.shape
    rows = attn_turned.shape[0]
    blocks = 8
    vmem = pl.BlockSpec(memory_space=pltpu.VMEM)
    anywhere = pl.BlockSpec(memory_space=pl.ANY)
    return pl.pallas_call(
        weight_kernel,
        out_shape=(
            jax.ShapeDtypeStruct((tokens, cols), BF16),
            jax.ShapeDtypeStruct((rows, cols), BF16),
        ),
        in_specs=[vmem] * 5,
        out_specs=(anywhere, anywhere),
        scratch_shapes=[
            pltpu.VMEM((tokens, cols), BF16),
            pltpu.VMEM((blocks, rows // blocks, cols), BF16),
            pltpu.SemaphoreType.DMA((blocks + 1,)),
        ],
        compiler_params=pltpu.CompilerParams(vmem_limit_bytes=VMEM_LIMIT),
        cost_estimate=pl.CostEstimate(
            flops=1100000000, bytes_accessed=7000000, transcendentals=0
        ),
    )(hidden, gained, rms, shrink, attn_turned)


def pool_sum_kernel(code_ref, weight_ref, q_ref, pool_ref, out_ref, spread_ref, held_ref, sems):
    blocks, block = held_ref.shape[0], held_ref.shape[2]
    copies = []
    for b in range(blocks):
        copy = pltpu.make_async_copy(
            q_ref.at[:, pl.ds(b * block, block)], held_ref.at[b], sems.at[b]
        )
        copy.start()
        copies.append(copy)
    group = LANES // WIDE
    steps = code_ref.shape[0] // group

    def lined(values):
        wide = tiled(values, WIDE, group)
        down = lax.broadcasted_iota(jnp.int32, wide.shape, 0)
        along = lax.broadcasted_iota(jnp.int32, wide.shape, 1)
        kept = jnp.where(along // WIDE == down % group, wide, 0.0)
        return jnp.sum(kept.reshape(wide.shape[0] // group, group, LANES), axis=1)

    code = code_ref[...]
    pool_row = lined(lax.shift_right_logical(code, 7).astype(F32)).astype(jnp.int32)
    query = lined(jnp.bitwise_and(code, 127).astype(F32)).astype(jnp.int32)
    peer = lax.broadcasted_iota(jnp.int32, (steps, LANES), 1) // WIDE
    query = jnp.where(query > 0, peer * Q_GRP + query - 1, -1)
    w_q = lined(weight_ref[:, :WIDE])
    w_n = lined(weight_ref[:, WIDE:])
    down = lax.broadcasted_iota(jnp.int32, (POOL_GRP, LANES), 0)
    across = lax.broadcasted_iota(jnp.int32, (group * Q_GRP, LANES), 0)
    own = jnp.zeros((POOL_GRP, LANES), F32)
    for step in range(steps):
        at = slice(step, step + 1)
        hot = down == pool_row[at]
        parts = split(jnp.where(hot, w_q[at], 0.0))
        pick = jnp.where(across == query[at], 1.0, 0.0).astype(BF16)
        spread_ref[:, step * group * Q_GRP : (step + 1) * group * Q_GRP] = dot(
            jnp.concatenate(parts, axis=0), pick, 1, 1
        ).astype(BF16)
        own += jnp.where(hot, w_n[at], 0.0)
    own = jnp.sum(own, axis=1, keepdims=True)
    for b in range(blocks):
        at = slice(b * block, (b + 1) * block)
        copies[b].wait()
        both = dot(spread_ref[...], held_ref[b], 1, 0)
        out_ref[:, at] = (
            both[:POOL_GRP] + both[POOL_GRP:] - own * pool_ref[:, at].astype(F32)
        ).astype(BF16)


def pool_sum(code, weights, q_all, pool):
    vmem = pl.BlockSpec(memory_space=pltpu.VMEM)
    return pl.pallas_call(
        pool_sum_kernel,
        out_shape=jax.ShapeDtypeStruct(pool.shape, BF16),
        in_specs=[vmem, vmem, pl.BlockSpec(memory_space=pl.ANY), vmem],
        out_specs=vmem,
        scratch_shapes=[
            pltpu.VMEM((2 * POOL_GRP, q_all.shape[0]), BF16),
            pltpu.VMEM((4, q_all.shape[0], pool.shape[1] // 4), BF16),
            pltpu.SemaphoreType.DMA((4,)),
        ],
        compiler_params=pltpu.CompilerParams(vmem_limit_bytes=60 * 1024 * 1024),
        cost_estimate=pl.CostEstimate(
            flops=2500000000, bytes_accessed=9000000, transcendentals=0
        ),
    )(code, weights, q_all, pool)


def per_device(q, pos, pool, neg_owner, neg_row, resid_in, attn_out, out_weight, norm_gain):
    owners = lax.axis_size("dp")
    cols = q.shape[1]
    tokens = resid_in.shape[0]

    q_all = lax.all_gather(q, "dp", tiled=True)

    code, slot, owner_turned, place_hot = request_tables(
        neg_owner.T * POOL_GRP + neg_row.T, owners
    )
    wanted = lax.all_to_all(code, "dp", split_axis=0, concat_axis=0, tiled=True)
    pool_tiles = pool.reshape(POOL_GRP, SUB, LANES)
    fetched = fetch_rows(wanted, pool_tiles).reshape(owners, SLOTS * SUB, LANES)
    replies = lax.all_to_all(fetched, "dp", split_axis=0, concat_axis=0, tiled=True)

    fetched, q, pos, resid_in, attn_out = lax.optimization_barrier(
        (fetched, q, pos, resid_in, attn_out)
    )
    attn_turned = attn_out.T
    hidden = resid_in.astype(F32) + dot(attn_out, out_weight, 1, 0)
    hid_hi, hid_lo = split(hidden)
    scaled = jnp.concatenate(split(hidden * norm_gain[None, :]), axis=0)
    both = jnp.concatenate([pos, q], axis=0)
    scaled_dots = dot(jnp.concatenate([pos, q[:CH_Q]], axis=0), scaled, 1, 1)
    early = feature_total(
        jnp.concatenate(
            [
                scaled_dots[:, :tokens] + scaled_dots[:, tokens:],
                jnp.concatenate([dot(q, both, 1, 1), dot(pos, both, 1, 1)], axis=1),
                jnp.broadcast_to(jnp.sum(hidden * hidden, axis=1)[None, :], (8, tokens)),
            ],
            axis=0,
        )
    )
    hidden_back = feature_scatter(dot(hid_hi, out_weight, 1, 1) + dot(hid_lo, out_weight, 1, 1))
    eye = jnp.eye(Q_GRP, dtype=F32)
    scaled_pos = early[:Q_GRP]
    mine = jnp.arange(CH_Q)[:, None] == (jnp.arange(tokens) // QLEN)[None, :]
    scaled_q = jnp.sum(jnp.where(mine, early[Q_GRP : Q_GRP + CH_Q], 0.0), axis=0)[None, :]
    pairs = early[Q_GRP + CH_Q : 2 * Q_GRP + CH_Q]
    q_sq = jnp.sum(pairs[:, Q_GRP : 2 * Q_GRP] * eye, axis=0)
    p_sq = jnp.sum(pairs[:, 2 * Q_GRP : 3 * Q_GRP] * eye, axis=0)
    h_sq = early[2 * Q_GRP + CH_Q]
    inv_q = lax.rsqrt(q_sq + rep_epsilon)
    inv_p = lax.rsqrt(p_sq + rep_epsilon)
    inv_rms = lax.rsqrt(h_sq / D + norm_epsilon)
    s_in = pairs[:, :Q_GRP] * inv_q[:, None] * inv_p[None, :] * inv_temp
    exp_in = jnp.exp(s_in)
    sum_in = jnp.sum(exp_in, axis=1)[None, :]
    inv_q_row = inv_q[None, :]
    inv_p_row = inv_p[None, :]
    rms_row = inv_rms[None, :]
    (
        replies, sum_in, inv_q_row, inv_p_row, rms_row, scaled, scaled_pos, scaled_q,
        attn_turned, hidden_back, exp_in, s_in, hidden,
    ) = lax.optimization_barrier(
        (
            replies, sum_in, inv_q_row, inv_p_row, rms_row, scaled, scaled_pos,
            scaled_q, attn_turned, hidden_back, exp_in, s_in, hidden,
        )
    )

    sums, first_negs = row_sums(
        slot, replies.reshape(owners * SLOTS, SUB, LANES), q.reshape(Q_GRP, SUB, LANES)
    )
    first_negs = first_negs.reshape(NEG * CH_Q, cols)
    scaled_negs = dot(first_negs, scaled, 1, 1)
    scaled_negs = (scaled_negs[:, :tokens] + scaled_negs[:, tokens:]).reshape(NEG, CH_Q, tokens)
    scaled_negs = jnp.sum(jnp.where(mine[None], scaled_negs, 0.0), axis=1)
    late = feature_total(
        jnp.concatenate(
            [sums[:SUB], sums[SUB:], jnp.concatenate([scaled_negs, jnp.zeros((1, tokens), F32)])],
            axis=1,
        )
    )
    sent, coef_neg, s_neg, inv_n, denominator = soft(
        late, sum_in, inv_q_row, owner_turned, place_hot
    )
    got = lax.all_to_all(sent, "dp", split_axis=0, concat_axis=0, tiled=True)

    gained, halves, shrink, pos_grad = grads(
        late, coef_neg, s_neg, inv_n, denominator, exp_in, s_in, inv_q_row, inv_p_row, rms_row,
        scaled_pos, scaled_q, norm_gain[None, :], q, pos, first_negs,
    )
    gained_back = dot(halves, out_weight, 1, 1)
    gained_back = feature_scatter_small(gained_back[:CH_Q] + gained_back[CH_Q:])
    resid_grad, weight_grad = weight_grads(hidden, gained, rms_row, shrink, attn_turned)
    own = tokens // N_FS
    first = lax.axis_index("fsdp") * own
    own_rms = lax.dynamic_slice(rms_row[0], (first,), (own,))
    own_shrink = lax.dynamic_slice(shrink[0], (first,), (own,))
    gained_rows = jnp.broadcast_to(
        gained_back[:, None, :], (CH_Q // N_FS, QLEN, gained_back.shape[1])
    ).reshape(own, gained_back.shape[1])
    attn_grad = (own_rms[:, None] * gained_rows - own_shrink[:, None] * hidden_back).astype(BF16)
    pool_grad = pool_sum(wanted, got, q_all, pool)
    return (
        resid_grad,
        attn_grad,
        weight_grad[None],
        pos_grad,
        pool_grad,
    )


def solution(mesh):
    placed = (
        P("dp", "fsdp"),
        P("dp", "fsdp"),
        P("dp", "fsdp"),
        P("dp", None),
        P("dp", None),
        P("dp", "fsdp"),
        P("dp", None),
        P(None, "fsdp"),
        P("fsdp"),
    )
    return jax.shard_map(
        per_device,
        mesh=mesh,
        in_specs=placed,
        out_specs=(
            P("dp", "fsdp"),
            P(("dp", "fsdp"), None),
            P("dp", None, "fsdp"),
            P("dp", "fsdp"),
            P("dp", "fsdp"),
        ),
        check_vma=False,
    )
```

```python
import jax
import jax.numpy as jnp
from jax import lax
from jax.experimental import pallas as pl
from jax.experimental.pallas import tpu as pltpu
from jax.sharding import PartitionSpec as P

D = 4096
NEG = 7
QLEN = 16
Q_GRP = 64
CH_Q = 16
POOL_GRP = 128
SLOTS = 14
WIDE = 16
SUB = 8
LANES = 128
VMEM_LIMIT = 24 * 1024 * 1024
N_FS = 4


inv_temp = 1.0 / 0.05
loss_scale = 32.0
rep_epsilon = 1e-06
norm_epsilon = 1e-05
F32 = jnp.float32
BF16 = jnp.bfloat16


def dot(a, b, ca, cb):
    return lax.dot_general(a, b, (((ca,), (cb,)), ((), ())), preferred_element_type=F32)


def dot_exact(a, b, ca, cb):
    return lax.dot_general(
        a, b, (((ca,), (cb,)), ((), ())), precision=lax.Precision.HIGHEST, preferred_element_type=F32
    )


def split(a):
    hi = a.astype(BF16)
    return hi, (a - hi.astype(F32)).astype(BF16)


def shifted(value, step):
    return lax.ppermute(value, "fsdp", [(i, (i + step) % N_FS) for i in range(N_FS)])


def swapped(value, mask):
    return lax.ppermute(value, "fsdp", [(i, i ^ mask) for i in range(N_FS)])


def feature_total(rows):
    return rows + shifted(rows, 1) + shifted(rows, 3) + shifted(rows, 2)


def feature_scatter_small(rows):
    own = rows.shape[0] // N_FS
    me = lax.axis_index("fsdp")
    half = me // 2
    mine = lax.dynamic_slice(rows, (half * 2 * own, 0), (2 * own, rows.shape[1]))
    other = lax.dynamic_slice(rows, ((1 - half) * 2 * own, 0), (2 * own, rows.shape[1]))
    mine = mine + swapped(other, 3)
    side = me % 2
    kept = lax.dynamic_slice(mine, (side * own, 0), (own, rows.shape[1]))
    given = lax.dynamic_slice(mine, ((1 - side) * own, 0), (own, rows.shape[1]))
    return kept + swapped(given, 1)


def feature_scatter(rows):
    own = rows.shape[0] // N_FS
    me = lax.axis_index("fsdp")
    total = lax.dynamic_slice(rows, (me * own, 0), (own, rows.shape[1]))
    for step in (1, 3, 2):
        there = lax.rem(me + step, N_FS)
        part = lax.dynamic_slice(rows, (there * own, 0), (own, rows.shape[1]))
        total += shifted(part.astype(BF16), step).astype(F32)
    return total


def eye_of(rows, cols):
    down = lax.broadcasted_iota(jnp.int32, (rows, cols), 0)
    return (down == lax.broadcasted_iota(jnp.int32, (rows, cols), 1)).astype(F32)


def to_column(row):
    size = row.shape[1]
    return jnp.sum(eye_of(size, size) * row, axis=1, keepdims=True)


def tiled(values, period, times):
    width = period * times
    down = lax.broadcasted_iota(jnp.int32, (period, width), 0)
    along = lax.broadcasted_iota(jnp.int32, (period, width), 1)
    return dot_exact(values, (along % period == down).astype(F32), 1, 0)


def flat_row(values, times):
    rows, period = values.shape
    wide = tiled(values, period, times)
    down = lax.broadcasted_iota(jnp.int32, wide.shape, 0)
    along = lax.broadcasted_iota(jnp.int32, wide.shape, 1)
    return jnp.sum(jnp.where(along // period == down, wide, 0.0), axis=0, keepdims=True)


def request_kernel(name_ref, code_ref, slot_ref, turned_ref, place_ref):
    name = flat_row(name_ref[...].astype(F32), NEG).astype(jnp.int32)
    owner = lax.shift_right_logical(name, 7).astype(F32)
    row = jnp.bitwise_and(name, 127).astype(F32)
    requests = owner.shape[1]
    peers = turned_ref.shape[0]
    along = lax.broadcasted_iota(jnp.int32, (1, requests), 1)
    down = lax.broadcasted_iota(jnp.int32, (peers, requests), 0)
    hot = jnp.where(down == owner.astype(jnp.int32), 1.0, 0.0)
    turned = hot.astype(BF16)
    earlier = lax.broadcasted_iota(jnp.int32, (requests, requests), 0) < along
    before = dot(turned, jnp.where(earlier, 1.0, 0.0).astype(BF16), 1, 0)
    position = jnp.sum(hot * before, axis=0, keepdims=True)
    down = lax.broadcasted_iota(jnp.int32, (WIDE, requests), 0)
    place = jnp.where(down == position.astype(jnp.int32), 1.0, 0.0)
    query = (along % Q_GRP + 1).astype(F32)
    marks = jnp.concatenate([place * row, place * query], axis=0).astype(BF16)
    table = dot(turned, marks, 1, 1).astype(jnp.int32)
    code_ref[...] = table[:, :WIDE] * 128 + table[:, WIDE:]
    slot_ref[...] = (owner * SLOTS + position).astype(jnp.int32)
    turned_ref[...] = turned
    place_ref[...] = place.astype(BF16)


def request_tables(name, owners):
    requests = name.shape[0] * name.shape[1]
    vmem = pl.BlockSpec(memory_space=pltpu.VMEM)
    return pl.pallas_call(
        request_kernel,
        out_shape=(
            jax.ShapeDtypeStruct((owners, WIDE), jnp.int32),
            jax.ShapeDtypeStruct((1, requests), jnp.int32),
            jax.ShapeDtypeStruct((owners, requests), BF16),
            jax.ShapeDtypeStruct((WIDE, requests), BF16),
        ),
        in_specs=[vmem],
        out_specs=(vmem,) * 4,
        compiler_params=pltpu.CompilerParams(vmem_limit_bytes=VMEM_LIMIT),
        cost_estimate=pl.CostEstimate(flops=30000000, bytes_accessed=100000, transcendentals=0),
    )(name)


def fetch_kernel(code_ref, pool_ref, out_ref):
    @pl.loop(0, out_ref.shape[0], unroll=2)
    def _(peer):
        for place in range(SLOTS):
            out_ref[peer, place] = pool_ref[lax.shift_right_logical(code_ref[peer, place], 7)]


def fetch_rows(code, pool_tiles):
    peers = code.shape[0]
    return pl.pallas_call(
        fetch_kernel,
        out_shape=jax.ShapeDtypeStruct((peers, SLOTS, SUB, LANES), BF16),
        in_specs=[
            pl.BlockSpec(memory_space=pltpu.SMEM),
            pl.BlockSpec(memory_space=pltpu.VMEM),
        ],
        out_specs=pl.BlockSpec(memory_space=pltpu.VMEM),
        compiler_params=pltpu.CompilerParams(vmem_limit_bytes=VMEM_LIMIT),
        cost_estimate=pl.CostEstimate(flops=0, bytes_accessed=2 * 1835008, transcendentals=0),
    )(code, pool_tiles)


def row_sums_kernel(slot_ref, reply_ref, q_ref, sums_ref, first_ref, cos_ref, sq_ref):
    last = reply_ref.shape[0] - 1

    def one(query, keep):
        asked = q_ref[query].astype(F32)
        for k in range(NEG):
            row = reply_ref[jnp.clip(slot_ref[0, k * Q_GRP + query], 0, last)]
            if keep:
                first_ref[k * CH_Q + query] = row
            wide = row.astype(F32)
            at = pl.ds(k * Q_GRP + query, 1)
            cos_ref[at, :] = jnp.sum(wide * asked, axis=0, keepdims=True)
            sq_ref[at, :] = jnp.sum(wide * wide, axis=0, keepdims=True)

    pl.loop(0, CH_Q, unroll=2)(lambda query: one(query, True))
    pl.loop(CH_Q, Q_GRP, unroll=4)(lambda query: one(query, False))

    line = lax.broadcasted_iota(jnp.int32, (SUB, LANES), 0)
    for part, ref in ((0, cos_ref), (1, sq_ref)):
        total = jnp.zeros((SUB, Q_GRP), F32)
        for k in range(NEG):
            total += dot_exact((line == k).astype(F32), ref[k * Q_GRP : (k + 1) * Q_GRP, :], 1, 1)
        sums_ref[part * SUB : (part + 1) * SUB, :] = total


def row_sums(slot, replies, q_tiles):
    return pl.pallas_call(
        row_sums_kernel,
        out_shape=(
            jax.ShapeDtypeStruct((2 * SUB, Q_GRP), F32),
            jax.ShapeDtypeStruct((NEG * CH_Q, SUB, LANES), BF16),
        ),
        in_specs=[
            pl.BlockSpec(memory_space=pltpu.SMEM),
            pl.BlockSpec(memory_space=pltpu.VMEM),
            pl.BlockSpec(memory_space=pltpu.VMEM),
        ],
        out_specs=(
            pl.BlockSpec(memory_space=pltpu.VMEM),
            pl.BlockSpec(memory_space=pltpu.VMEM),
        ),
        scratch_shapes=[
            pltpu.VMEM((NEG * Q_GRP, LANES), F32),
            pltpu.VMEM((NEG * Q_GRP, LANES), F32),
        ],
        compiler_params=pltpu.CompilerParams(vmem_limit_bytes=VMEM_LIMIT),
        cost_estimate=pl.CostEstimate(flops=2000000, bytes_accessed=2200000, transcendentals=0),
    )(slot, replies, q_tiles)


def soft_kernel(
    late_ref, sum_ref, inv_q_ref, owner_ref, place_ref, sent_ref, coef_ref, logit_ref, inv_n_ref, den_ref
):
    late = late_ref[...]
    inv_q = inv_q_ref[...]
    inv_n = lax.rsqrt(late[:, Q_GRP : 2 * Q_GRP] + rep_epsilon)
    logit = late[:, :Q_GRP] * inv_q * inv_n * inv_temp
    used = lax.broadcasted_iota(jnp.int32, logit.shape, 0) < NEG
    raised = jnp.where(used, jnp.exp(logit), 0.0)
    total = sum_ref[...] + jnp.sum(raised, axis=0, keepdims=True)
    coef = raised / total
    coef_ref[...] = coef
    logit_ref[...] = logit
    inv_n_ref[...] = inv_n
    den_ref[...] = total
    w_q = flat_row(loss_scale * inv_temp * coef * inv_q * inv_n, NEG)
    w_n = flat_row(loss_scale * coef * logit * inv_n * inv_n, NEG)
    owner = owner_ref[...].astype(F32)
    parts = split(owner * w_q) + split(owner * w_n)
    placed = dot(jnp.concatenate(parts, axis=0), place_ref[...], 1, 1)
    peers = owner.shape[0]
    sent_ref[:, :WIDE] = placed[:peers] + placed[peers : 2 * peers]
    sent_ref[:, WIDE:] = placed[2 * peers : 3 * peers] + placed[3 * peers :]


def soft(late, sum_in, inv_q, owner_turned, place_hot):
    small = jax.ShapeDtypeStruct((SUB, Q_GRP), F32)
    vmem = pl.BlockSpec(memory_space=pltpu.VMEM)
    return pl.pallas_call(
        soft_kernel,
        out_shape=(
            jax.ShapeDtypeStruct((owner_turned.shape[0], 2 * WIDE), F32),
            small,
            small,
            small,
            jax.ShapeDtypeStruct((1, Q_GRP), F32),
        ),
        in_specs=[vmem] * 5,
        out_specs=(vmem,) * 5,
        compiler_params=pltpu.CompilerParams(vmem_limit_bytes=VMEM_LIMIT),
        cost_estimate=pl.CostEstimate(flops=8000000, bytes_accessed=100000, transcendentals=512),
    )(late, sum_in, inv_q, owner_turned, place_hot)


def grads_kernel(
    late_ref, coef_ref, logit_ref, inv_n_ref, den_ref, exp_ref, s_ref, inv_q_ref, inv_p_ref,
    rms_ref, scaled_pos_ref, scaled_q_ref, gain_ref, q_ref, pos_ref, negs_ref,
    gained_ref, halves_ref, shrink_ref, pos_grad_ref,
):
    eye = eye_of(Q_GRP, Q_GRP)
    inv_q_row = inv_q_ref[...]
    inv_p_row = inv_p_ref[...]
    inv_q = to_column(inv_q_row)
    coef_neg = coef_ref[...]
    coef_in = exp_ref[...] / to_column(den_ref[...]) - eye
    product = coef_in * s_ref[...]
    neg_dot = jnp.sum(coef_neg * logit_ref[...], axis=0, keepdims=True)
    self_dot = loss_scale * (jnp.sum(product, axis=1, keepdims=True) + to_column(neg_dot))
    scale_dir = loss_scale * inv_temp / QLEN * inv_q
    scale_own = inv_q * inv_q * self_dot * (1.0 / QLEN)
    of_pos = (coef_in * inv_p_row * scale_dir)[:CH_Q]
    neg_part = (coef_neg * inv_n_ref[...] * (loss_scale * inv_temp / QLEN) * inv_q_row)[:, :CH_Q]
    neg_row = flat_row(neg_part, NEG)
    down = lax.broadcasted_iota(jnp.int32, (CH_Q, NEG * CH_Q), 0)
    along = lax.broadcasted_iota(jnp.int32, (CH_Q, NEG * CH_Q), 1)
    of_neg = jnp.where(along % CH_Q == down, neg_row, 0.0)
    of_own = -eye[:CH_Q, :CH_Q] * scale_own[:CH_Q]
    both = (
        dot(jnp.concatenate(split(of_pos), axis=0), pos_ref[...], 1, 0)
        + dot(jnp.concatenate(split(of_neg), axis=0), negs_ref[...], 1, 0)
        + dot(jnp.concatenate(split(of_own), axis=0), q_ref[:CH_Q, :], 1, 0)
    )
    gained = (both[:CH_Q] + both[CH_Q:]) * gain_ref[...]
    gained_ref[...] = gained
    high, low = split(gained)
    halves_ref[:CH_Q, :] = high
    halves_ref[CH_Q:, :] = low
    tokens = CH_Q * QLEN
    down = lax.broadcasted_iota(jnp.int32, (CH_Q, tokens), 0)
    mine = lax.broadcasted_iota(jnp.int32, (CH_Q, tokens), 1) // QLEN == down
    inner = dot_exact(of_pos, scaled_pos_ref[...], 1, 0) - scale_own[:CH_Q] * scaled_q_ref[...]
    inner = jnp.sum(jnp.where(mine, inner, 0.0), axis=0, keepdims=True)
    spread = dot_exact(neg_part, mine.astype(F32), 1, 0)
    inner += jnp.sum(spread * late_ref[:, 2 * Q_GRP :], axis=0, keepdims=True)
    rms = rms_ref[...]
    shrink_ref[...] = rms * rms * rms * inner * (1.0 / D)
    back = coef_in * inv_q * (inv_p_row * (loss_scale * inv_temp))
    turned = dot(jnp.concatenate(split(back), axis=1), q_ref[...], 0, 0)
    less = to_column(inv_p_row * inv_p_row * loss_scale * jnp.sum(product, axis=0, keepdims=True))
    pos_grad_ref[...] = (
        turned[:Q_GRP] + turned[Q_GRP:] - less * pos_ref[...].astype(F32)
    ).astype(BF16)


def grads(*operands):
    vmem = pl.BlockSpec(memory_space=pltpu.VMEM)
    cols = operands[-1].shape[1]
    return pl.pallas_call(
        grads_kernel,
        out_shape=(
            jax.ShapeDtypeStruct((CH_Q, cols), F32),
            jax.ShapeDtypeStruct((2 * CH_Q, cols), BF16),
            jax.ShapeDtypeStruct((1, CH_Q * QLEN), F32),
            jax.ShapeDtypeStruct((Q_GRP, cols), BF16),
        ),
        in_specs=[vmem] * len(operands),
        out_specs=(vmem,) * 4,
        compiler_params=pltpu.CompilerParams(vmem_limit_bytes=VMEM_LIMIT),
        cost_estimate=pl.CostEstimate(flops=40000000, bytes_accessed=1000000, transcendentals=0),
    )(*operands)


def weight_kernel(
    hidden_ref, gained_ref, rms_ref, shrink_ref, attn_ref, resid_ref, out_ref, held_ref, tile_ref, sems
):
    rms = to_column(rms_ref[...])
    shrink = to_column(shrink_ref[...])
    for c in range(CH_Q):
        at = slice(c * QLEN, (c + 1) * QLEN)
        held_ref[at, :] = (
            rms[at] * gained_ref[c : c + 1, :] - shrink[at] * hidden_ref[at, :]
        ).astype(BF16)
    blocks, block = tile_ref.shape[0], tile_ref.shape[1]
    copies = [pltpu.make_async_copy(held_ref, resid_ref, sems.at[blocks])]
    copies[0].start()
    for b in range(blocks):
        at = slice(b * block, (b + 1) * block)
        tile_ref[b] = dot(attn_ref[at, :], held_ref[...], 1, 0).astype(BF16)
        copy = pltpu.make_async_copy(tile_ref.at[b], out_ref.at[pl.ds(b * block, block)], sems.at[b])
        copy.start()
        copies.append(copy)
    for copy in copies:
        copy.wait()


def weight_grads(hidden, gained, rms, shrink, attn_turned):
    tokens, cols = hidden.shape
    rows = attn_turned.shape[0]
    blocks = 8
    vmem = pl.BlockSpec(memory_space=pltpu.VMEM)
    anywhere = pl.BlockSpec(memory_space=pl.ANY)
    return pl.pallas_call(
        weight_kernel,
        out_shape=(
            jax.ShapeDtypeStruct((tokens, cols), BF16),
            jax.ShapeDtypeStruct((rows, cols), BF16),
        ),
        in_specs=[vmem] * 5,
        out_specs=(anywhere, anywhere),
        scratch_shapes=[
            pltpu.VMEM((tokens, cols), BF16),
            pltpu.VMEM((blocks, rows // blocks, cols), BF16),
            pltpu.SemaphoreType.DMA((blocks + 1,)),
        ],
        compiler_params=pltpu.CompilerParams(vmem_limit_bytes=VMEM_LIMIT),
        cost_estimate=pl.CostEstimate(
            flops=1100000000, bytes_accessed=7000000, transcendentals=0
        ),
    )(hidden, gained, rms, shrink, attn_turned)


def pool_sum_kernel(code_ref, weight_ref, q_ref, pool_ref, out_ref, spread_ref):
    group = LANES // WIDE
    steps = code_ref.shape[0] // group

    def lined(values):
        wide = tiled(values, WIDE, group)
        down = lax.broadcasted_iota(jnp.int32, wide.shape, 0)
        along = lax.broadcasted_iota(jnp.int32, wide.shape, 1)
        kept = jnp.where(along // WIDE == down % group, wide, 0.0)
        return jnp.sum(kept.reshape(wide.shape[0] // group, group, LANES), axis=1)

    code = code_ref[...]
    pool_row = lined(lax.shift_right_logical(code, 7).astype(F32)).astype(jnp.int32)
    query = lined(jnp.bitwise_and(code, 127).astype(F32)).astype(jnp.int32)
    peer = lax.broadcasted_iota(jnp.int32, (steps, LANES), 1) // WIDE
    query = jnp.where(query > 0, peer * Q_GRP + query - 1, -1)
    w_q = lined(weight_ref[:, :WIDE])
    w_n = lined(weight_ref[:, WIDE:])
    down = lax.broadcasted_iota(jnp.int32, (POOL_GRP, LANES), 0)
    across = lax.broadcasted_iota(jnp.int32, (group * Q_GRP, LANES), 0)
    own = jnp.zeros((POOL_GRP, LANES), F32)
    for step in range(steps):
        at = slice(step, step + 1)
        hot = down == pool_row[at]
        parts = split(jnp.where(hot, w_q[at], 0.0))
        pick = jnp.where(across == query[at], 1.0, 0.0).astype(BF16)
        spread_ref[:, step * group * Q_GRP : (step + 1) * group * Q_GRP] = dot(
            jnp.concatenate(parts, axis=0), pick, 1, 1
        ).astype(BF16)
        own += jnp.where(hot, w_n[at], 0.0)
    own = jnp.sum(own, axis=1, keepdims=True)
    width = 256
    for first in range(0, out_ref.shape[1], width):
        at = slice(first, first + width)
        both = dot(spread_ref[...], q_ref[:, at], 1, 0)
        out_ref[:, at] = (
            both[:POOL_GRP] + both[POOL_GRP:] - own * pool_ref[:, at].astype(F32)
        ).astype(BF16)


def pool_sum(code, weights, q_all, pool):
    vmem = pl.BlockSpec(memory_space=pltpu.VMEM)
    return pl.pallas_call(
        pool_sum_kernel,
        out_shape=jax.ShapeDtypeStruct(pool.shape, BF16),
        in_specs=[vmem] * 4,
        out_specs=vmem,
        scratch_shapes=[pltpu.VMEM((2 * POOL_GRP, q_all.shape[0]), BF16)],
        compiler_params=pltpu.CompilerParams(vmem_limit_bytes=VMEM_LIMIT),
        cost_estimate=pl.CostEstimate(
            flops=2500000000, bytes_accessed=9000000, transcendentals=0
        ),
    )(code, weights, q_all, pool)


def per_device(q, pos, pool, neg_owner, neg_row, resid_in, attn_out, out_weight, norm_gain):
    owners = lax.axis_size("dp")
    cols = q.shape[1]
    tokens = resid_in.shape[0]

    q_all = lax.all_gather(q, "dp", tiled=True)

    code, slot, owner_turned, place_hot = request_tables(
        neg_owner.T * POOL_GRP + neg_row.T, owners
    )
    wanted = lax.all_to_all(code, "dp", split_axis=0, concat_axis=0, tiled=True)
    pool_tiles = pool.reshape(POOL_GRP, SUB, LANES)
    fetched = fetch_rows(wanted, pool_tiles).reshape(owners, SLOTS * SUB, LANES)
    replies = lax.all_to_all(fetched, "dp", split_axis=0, concat_axis=0, tiled=True)

    fetched, q, pos, resid_in, attn_out = lax.optimization_barrier(
        (fetched, q, pos, resid_in, attn_out)
    )
    attn_turned = attn_out.T
    hidden = resid_in.astype(F32) + dot(attn_out, out_weight, 1, 0)
    hid_hi, hid_lo = split(hidden)
    scaled = jnp.concatenate(split(hidden * norm_gain[None, :]), axis=0)
    both = jnp.concatenate([pos, q], axis=0)
    scaled_dots = dot(jnp.concatenate([pos, q[:CH_Q]], axis=0), scaled, 1, 1)
    early = feature_total(
        jnp.concatenate(
            [
                scaled_dots[:, :tokens] + scaled_dots[:, tokens:],
                jnp.concatenate([dot(q, both, 1, 1), dot(pos, both, 1, 1)], axis=1),
                jnp.broadcast_to(jnp.sum(hidden * hidden, axis=1)[None, :], (8, tokens)),
            ],
            axis=0,
        )
    )
    hidden_back = feature_scatter(dot(hid_hi, out_weight, 1, 1) + dot(hid_lo, out_weight, 1, 1))
    eye = jnp.eye(Q_GRP, dtype=F32)
    scaled_pos = early[:Q_GRP]
    mine = jnp.arange(CH_Q)[:, None] == (jnp.arange(tokens) // QLEN)[None, :]
    scaled_q = jnp.sum(jnp.where(mine, early[Q_GRP : Q_GRP + CH_Q], 0.0), axis=0)[None, :]
    pairs = early[Q_GRP + CH_Q : 2 * Q_GRP + CH_Q]
    q_sq = jnp.sum(pairs[:, Q_GRP : 2 * Q_GRP] * eye, axis=0)
    p_sq = jnp.sum(pairs[:, 2 * Q_GRP : 3 * Q_GRP] * eye, axis=0)
    h_sq = early[2 * Q_GRP + CH_Q]
    inv_q = lax.rsqrt(q_sq + rep_epsilon)
    inv_p = lax.rsqrt(p_sq + rep_epsilon)
    inv_rms = lax.rsqrt(h_sq / D + norm_epsilon)
    s_in = pairs[:, :Q_GRP] * inv_q[:, None] * inv_p[None, :] * inv_temp
    exp_in = jnp.exp(s_in)
    sum_in = jnp.sum(exp_in, axis=1)[None, :]
    inv_q_row = inv_q[None, :]
    inv_p_row = inv_p[None, :]
    rms_row = inv_rms[None, :]
    (
        replies, sum_in, inv_q_row, inv_p_row, rms_row, scaled, scaled_pos, scaled_q,
        attn_turned, hidden_back, exp_in, s_in, hidden,
    ) = lax.optimization_barrier(
        (
            replies, sum_in, inv_q_row, inv_p_row, rms_row, scaled, scaled_pos,
            scaled_q, attn_turned, hidden_back, exp_in, s_in, hidden,
        )
    )

    sums, first_negs = row_sums(
        slot, replies.reshape(owners * SLOTS, SUB, LANES), q.reshape(Q_GRP, SUB, LANES)
    )
    first_negs = first_negs.reshape(NEG * CH_Q, cols)
    scaled_negs = dot(first_negs, scaled, 1, 1)
    scaled_negs = (scaled_negs[:, :tokens] + scaled_negs[:, tokens:]).reshape(NEG, CH_Q, tokens)
    scaled_negs = jnp.sum(jnp.where(mine[None], scaled_negs, 0.0), axis=1)
    late = feature_total(
        jnp.concatenate(
            [sums[:SUB], sums[SUB:], jnp.concatenate([scaled_negs, jnp.zeros((1, tokens), F32)])],
            axis=1,
        )
    )
    sent, coef_neg, s_neg, inv_n, denominator = soft(
        late, sum_in, inv_q_row, owner_turned, place_hot
    )
    got = lax.all_to_all(sent, "dp", split_axis=0, concat_axis=0, tiled=True)

    gained, halves, shrink, pos_grad = grads(
        late, coef_neg, s_neg, inv_n, denominator, exp_in, s_in, inv_q_row, inv_p_row, rms_row,
        scaled_pos, scaled_q, norm_gain[None, :], q, pos, first_negs,
    )
    gained_back = dot(halves, out_weight, 1, 1)
    gained_back = feature_scatter_small(gained_back[:CH_Q] + gained_back[CH_Q:])
    resid_grad, weight_grad = weight_grads(hidden, gained, rms_row, shrink, attn_turned)
    own = tokens // N_FS
    first = lax.axis_index("fsdp") * own
    own_rms = lax.dynamic_slice(rms_row[0], (first,), (own,))
    own_shrink = lax.dynamic_slice(shrink[0], (first,), (own,))
    gained_rows = jnp.broadcast_to(
        gained_back[:, None, :], (CH_Q // N_FS, QLEN, gained_back.shape[1])
    ).reshape(own, gained_back.shape[1])
    attn_grad = (own_rms[:, None] * gained_rows - own_shrink[:, None] * hidden_back).astype(BF16)
    pool_grad = pool_sum(wanted, got, q_all, pool)
    return (
        resid_grad,
        attn_grad,
        weight_grad[None],
        pos_grad,
        pool_grad,
    )


def solution(mesh):
    placed = (
        P("dp", "fsdp"),
        P("dp", "fsdp"),
        P("dp", "fsdp"),
        P("dp", None),
        P("dp", None),
        P("dp", "fsdp"),
        P("dp", None),
        P(None, "fsdp"),
        P("fsdp"),
    )
    return jax.shard_map(
        per_device,
        mesh=mesh,
        in_specs=placed,
        out_specs=(
            P("dp", "fsdp"),
            P(("dp", "fsdp"), None),
            P("dp", None, "fsdp"),
            P("dp", "fsdp"),
            P("dp", "fsdp"),
        ),
        check_vma=False,
    )
```

```python
import jax
import jax.numpy as jnp
from jax import lax
from jax.experimental import pallas as pl
from jax.experimental.pallas import tpu as pltpu
from jax.sharding import PartitionSpec as P

D = 4096
NEG = 7
QLEN = 16
Q_GRP = 64
CH_Q = 16
POOL_GRP = 128
SLOTS = 14
WIDE = 16
SUB = 8
LANES = 128
VMEM_LIMIT = 24 * 1024 * 1024
N_FS = 4


inv_temp = 1.0 / 0.05
loss_scale = 32.0
rep_epsilon = 1e-06
norm_epsilon = 1e-05
F32 = jnp.float32
BF16 = jnp.bfloat16


def dot(a, b, ca, cb):
    return lax.dot_general(a, b, (((ca,), (cb,)), ((), ())), preferred_element_type=F32)


def dot_exact(a, b, ca, cb):
    return lax.dot_general(
        a, b, (((ca,), (cb,)), ((), ())), precision=lax.Precision.HIGHEST, preferred_element_type=F32
    )


def split(a):
    hi = a.astype(BF16)
    return hi, (a - hi.astype(F32)).astype(BF16)


def shifted(value, step):
    return lax.ppermute(value, "fsdp", [(i, (i + step) % N_FS) for i in range(N_FS)])


def swapped(value, mask):
    return lax.ppermute(value, "fsdp", [(i, i ^ mask) for i in range(N_FS)])


def feature_total(rows):
    return rows + shifted(rows, 1) + shifted(rows, 3) + shifted(rows, 2)


def feature_scatter_small(rows):
    own = rows.shape[0] // N_FS
    me = lax.axis_index("fsdp")
    half = me // 2
    mine = lax.dynamic_slice(rows, (half * 2 * own, 0), (2 * own, rows.shape[1]))
    other = lax.dynamic_slice(rows, ((1 - half) * 2 * own, 0), (2 * own, rows.shape[1]))
    mine = mine + swapped(other, 3)
    side = me % 2
    kept = lax.dynamic_slice(mine, (side * own, 0), (own, rows.shape[1]))
    given = lax.dynamic_slice(mine, ((1 - side) * own, 0), (own, rows.shape[1]))
    return kept + swapped(given, 1)


def feature_scatter(rows):
    own = rows.shape[0] // N_FS
    me = lax.axis_index("fsdp")
    total = lax.dynamic_slice(rows, (me * own, 0), (own, rows.shape[1]))
    for step in (1, 3, 2):
        there = lax.rem(me + step, N_FS)
        part = lax.dynamic_slice(rows, (there * own, 0), (own, rows.shape[1]))
        total += shifted(part.astype(BF16), step).astype(F32)
    return total


def eye_of(rows, cols):
    down = lax.broadcasted_iota(jnp.int32, (rows, cols), 0)
    return (down == lax.broadcasted_iota(jnp.int32, (rows, cols), 1)).astype(F32)


def to_column(row):
    size = row.shape[1]
    return jnp.sum(eye_of(size, size) * row, axis=1, keepdims=True)


def tiled(values, period, times):
    width = period * times
    down = lax.broadcasted_iota(jnp.int32, (period, width), 0)
    along = lax.broadcasted_iota(jnp.int32, (period, width), 1)
    return dot_exact(values, (along % period == down).astype(F32), 1, 0)


def flat_row(values, times):
    rows, period = values.shape
    wide = tiled(values, period, times)
    down = lax.broadcasted_iota(jnp.int32, wide.shape, 0)
    along = lax.broadcasted_iota(jnp.int32, wide.shape, 1)
    return jnp.sum(jnp.where(along // period == down, wide, 0.0), axis=0, keepdims=True)


def request_kernel(name_ref, code_ref, slot_ref, turned_ref, place_ref):
    name = flat_row(name_ref[...].astype(F32), NEG).astype(jnp.int32)
    owner = lax.shift_right_logical(name, 7).astype(F32)
    row = jnp.bitwise_and(name, 127).astype(F32)
    requests = owner.shape[1]
    peers = turned_ref.shape[0]
    along = lax.broadcasted_iota(jnp.int32, (1, requests), 1)
    down = lax.broadcasted_iota(jnp.int32, (peers, requests), 0)
    hot = jnp.where(down == owner.astype(jnp.int32), 1.0, 0.0)
    turned = hot.astype(BF16)
    earlier = lax.broadcasted_iota(jnp.int32, (requests, requests), 0) < along
    before = dot(turned, jnp.where(earlier, 1.0, 0.0).astype(BF16), 1, 0)
    position = jnp.sum(hot * before, axis=0, keepdims=True)
    down = lax.broadcasted_iota(jnp.int32, (WIDE, requests), 0)
    place = jnp.where(down == position.astype(jnp.int32), 1.0, 0.0)
    query = (along % Q_GRP + 1).astype(F32)
    marks = jnp.concatenate([place * row, place * query], axis=0).astype(BF16)
    table = dot(turned, marks, 1, 1).astype(jnp.int32)
    code_ref[...] = table[:, :WIDE] * 128 + table[:, WIDE:]
    slot_ref[...] = (owner * SLOTS + position).astype(jnp.int32)
    turned_ref[...] = turned
    place_ref[...] = place.astype(BF16)


def request_tables(name, owners):
    requests = name.shape[0] * name.shape[1]
    vmem = pl.BlockSpec(memory_space=pltpu.VMEM)
    return pl.pallas_call(
        request_kernel,
        out_shape=(
            jax.ShapeDtypeStruct((owners, WIDE), jnp.int32),
            jax.ShapeDtypeStruct((1, requests), jnp.int32),
            jax.ShapeDtypeStruct((owners, requests), BF16),
            jax.ShapeDtypeStruct((WIDE, requests), BF16),
        ),
        in_specs=[vmem],
        out_specs=(vmem,) * 4,
        compiler_params=pltpu.CompilerParams(vmem_limit_bytes=VMEM_LIMIT),
        cost_estimate=pl.CostEstimate(flops=30000000, bytes_accessed=100000, transcendentals=0),
    )(name)


def fetch_kernel(code_ref, pool_ref, out_ref):
    @pl.loop(0, out_ref.shape[0], unroll=2)
    def _(peer):
        for place in range(SLOTS):
            out_ref[peer, place] = pool_ref[lax.shift_right_logical(code_ref[peer, place], 7)]


def fetch_rows(code, pool_tiles):
    peers = code.shape[0]
    return pl.pallas_call(
        fetch_kernel,
        out_shape=jax.ShapeDtypeStruct((peers, SLOTS, SUB, LANES), BF16),
        in_specs=[
            pl.BlockSpec(memory_space=pltpu.SMEM),
            pl.BlockSpec(memory_space=pltpu.VMEM),
        ],
        out_specs=pl.BlockSpec(memory_space=pltpu.VMEM),
        compiler_params=pltpu.CompilerParams(vmem_limit_bytes=VMEM_LIMIT),
        cost_estimate=pl.CostEstimate(flops=0, bytes_accessed=2 * 1835008, transcendentals=0),
    )(code, pool_tiles)


def row_sums_kernel(slot_ref, reply_ref, q_ref, sums_ref, first_ref, cos_ref, sq_ref):
    last = reply_ref.shape[0] - 1

    def one(query, keep):
        asked = q_ref[query].astype(F32)
        for k in range(NEG):
            row = reply_ref[jnp.clip(slot_ref[0, k * Q_GRP + query], 0, last)]
            if keep:
                first_ref[k * CH_Q + query] = row
            wide = row.astype(F32)
            at = pl.ds(k * Q_GRP + query, 1)
            cos_ref[at, :] = jnp.sum(wide * asked, axis=0, keepdims=True)
            sq_ref[at, :] = jnp.sum(wide * wide, axis=0, keepdims=True)

    pl.loop(0, CH_Q, unroll=2)(lambda query: one(query, True))
    pl.loop(CH_Q, Q_GRP, unroll=4)(lambda query: one(query, False))

    line = lax.broadcasted_iota(jnp.int32, (SUB, LANES), 0)
    for part, ref in ((0, cos_ref), (1, sq_ref)):
        total = jnp.zeros((SUB, Q_GRP), F32)
        for k in range(NEG):
            total += dot_exact((line == k).astype(F32), ref[k * Q_GRP : (k + 1) * Q_GRP, :], 1, 1)
        sums_ref[part * SUB : (part + 1) * SUB, :] = total


def row_sums(slot, replies, q_tiles):
    return pl.pallas_call(
        row_sums_kernel,
        out_shape=(
            jax.ShapeDtypeStruct((2 * SUB, Q_GRP), F32),
            jax.ShapeDtypeStruct((NEG * CH_Q, SUB, LANES), BF16),
        ),
        in_specs=[
            pl.BlockSpec(memory_space=pltpu.SMEM),
            pl.BlockSpec(memory_space=pltpu.VMEM),
            pl.BlockSpec(memory_space=pltpu.VMEM),
        ],
        out_specs=(
            pl.BlockSpec(memory_space=pltpu.VMEM),
            pl.BlockSpec(memory_space=pltpu.VMEM),
        ),
        scratch_shapes=[
            pltpu.VMEM((NEG * Q_GRP, LANES), F32),
            pltpu.VMEM((NEG * Q_GRP, LANES), F32),
        ],
        compiler_params=pltpu.CompilerParams(vmem_limit_bytes=VMEM_LIMIT),
        cost_estimate=pl.CostEstimate(flops=2000000, bytes_accessed=2200000, transcendentals=0),
    )(slot, replies, q_tiles)


def soft_kernel(
    late_ref, sum_ref, inv_q_ref, owner_ref, place_ref, sent_ref, coef_ref, logit_ref, inv_n_ref, den_ref
):
    late = late_ref[...]
    inv_q = inv_q_ref[...]
    inv_n = lax.rsqrt(late[:, Q_GRP : 2 * Q_GRP] + rep_epsilon)
    logit = late[:, :Q_GRP] * inv_q * inv_n * inv_temp
    used = lax.broadcasted_iota(jnp.int32, logit.shape, 0) < NEG
    raised = jnp.where(used, jnp.exp(logit), 0.0)
    total = sum_ref[...] + jnp.sum(raised, axis=0, keepdims=True)
    coef = raised / total
    coef_ref[...] = coef
    logit_ref[...] = logit
    inv_n_ref[...] = inv_n
    den_ref[...] = total
    w_q = flat_row(loss_scale * inv_temp * coef * inv_q * inv_n, NEG)
    w_n = flat_row(loss_scale * coef * logit * inv_n * inv_n, NEG)
    owner = owner_ref[...].astype(F32)
    parts = split(owner * w_q) + split(owner * w_n)
    placed = dot(jnp.concatenate(parts, axis=0), place_ref[...], 1, 1)
    peers = owner.shape[0]
    sent_ref[:, :WIDE] = placed[:peers] + placed[peers : 2 * peers]
    sent_ref[:, WIDE:] = placed[2 * peers : 3 * peers] + placed[3 * peers :]


def soft(late, sum_in, inv_q, owner_turned, place_hot):
    small = jax.ShapeDtypeStruct((SUB, Q_GRP), F32)
    vmem = pl.BlockSpec(memory_space=pltpu.VMEM)
    return pl.pallas_call(
        soft_kernel,
        out_shape=(
            jax.ShapeDtypeStruct((owner_turned.shape[0], 2 * WIDE), F32),
            small,
            small,
            small,
            jax.ShapeDtypeStruct((1, Q_GRP), F32),
        ),
        in_specs=[vmem] * 5,
        out_specs=(vmem,) * 5,
        compiler_params=pltpu.CompilerParams(vmem_limit_bytes=VMEM_LIMIT),
        cost_estimate=pl.CostEstimate(flops=8000000, bytes_accessed=100000, transcendentals=512),
    )(late, sum_in, inv_q, owner_turned, place_hot)


def grads_kernel(
    late_ref, coef_ref, logit_ref, inv_n_ref, den_ref, exp_ref, s_ref, inv_q_ref, inv_p_ref,
    rms_ref, scaled_pos_ref, scaled_q_ref, gain_ref, q_ref, pos_ref, negs_ref,
    gained_ref, halves_ref, shrink_ref, pos_grad_ref,
):
    eye = eye_of(Q_GRP, Q_GRP)
    inv_q_row = inv_q_ref[...]
    inv_p_row = inv_p_ref[...]
    inv_q = to_column(inv_q_row)
    coef_neg = coef_ref[...]
    coef_in = exp_ref[...] / to_column(den_ref[...]) - eye
    product = coef_in * s_ref[...]
    neg_dot = jnp.sum(coef_neg * logit_ref[...], axis=0, keepdims=True)
    self_dot = loss_scale * (jnp.sum(product, axis=1, keepdims=True) + to_column(neg_dot))
    scale_dir = loss_scale * inv_temp / QLEN * inv_q
    scale_own = inv_q * inv_q * self_dot * (1.0 / QLEN)
    of_pos = (coef_in * inv_p_row * scale_dir)[:CH_Q]
    neg_part = (coef_neg * inv_n_ref[...] * (loss_scale * inv_temp / QLEN) * inv_q_row)[:, :CH_Q]
    neg_row = flat_row(neg_part, NEG)
    down = lax.broadcasted_iota(jnp.int32, (CH_Q, NEG * CH_Q), 0)
    along = lax.broadcasted_iota(jnp.int32, (CH_Q, NEG * CH_Q), 1)
    of_neg = jnp.where(along % CH_Q == down, neg_row, 0.0)
    of_own = -eye[:CH_Q, :CH_Q] * scale_own[:CH_Q]
    both = (
        dot(jnp.concatenate(split(of_pos), axis=0), pos_ref[...], 1, 0)
        + dot(jnp.concatenate(split(of_neg), axis=0), negs_ref[...], 1, 0)
        + dot(jnp.concatenate(split(of_own), axis=0), q_ref[:CH_Q, :], 1, 0)
    )
    gained = (both[:CH_Q] + both[CH_Q:]) * gain_ref[...]
    gained_ref[...] = gained
    high, low = split(gained)
    halves_ref[:CH_Q, :] = high
    halves_ref[CH_Q:, :] = low
    tokens = CH_Q * QLEN
    down = lax.broadcasted_iota(jnp.int32, (CH_Q, tokens), 0)
    mine = lax.broadcasted_iota(jnp.int32, (CH_Q, tokens), 1) // QLEN == down
    inner = dot_exact(of_pos, scaled_pos_ref[...], 1, 0) - scale_own[:CH_Q] * scaled_q_ref[...]
    inner = jnp.sum(jnp.where(mine, inner, 0.0), axis=0, keepdims=True)
    spread = dot_exact(neg_part, mine.astype(F32), 1, 0)
    inner += jnp.sum(spread * late_ref[:, 2 * Q_GRP :], axis=0, keepdims=True)
    rms = rms_ref[...]
    shrink_ref[...] = rms * rms * rms * inner * (1.0 / D)
    back = coef_in * inv_q * (inv_p_row * (loss_scale * inv_temp))
    turned = dot(jnp.concatenate(split(back), axis=1), q_ref[...], 0, 0)
    less = to_column(inv_p_row * inv_p_row * loss_scale * jnp.sum(product, axis=0, keepdims=True))
    pos_grad_ref[...] = (
        turned[:Q_GRP] + turned[Q_GRP:] - less * pos_ref[...].astype(F32)
    ).astype(BF16)


def grads(*operands):
    vmem = pl.BlockSpec(memory_space=pltpu.VMEM)
    cols = operands[-1].shape[1]
    return pl.pallas_call(
        grads_kernel,
        out_shape=(
            jax.ShapeDtypeStruct((CH_Q, cols), F32),
            jax.ShapeDtypeStruct((2 * CH_Q, cols), BF16),
            jax.ShapeDtypeStruct((1, CH_Q * QLEN), F32),
            jax.ShapeDtypeStruct((Q_GRP, cols), BF16),
        ),
        in_specs=[vmem] * len(operands),
        out_specs=(vmem,) * 4,
        compiler_params=pltpu.CompilerParams(vmem_limit_bytes=VMEM_LIMIT),
        cost_estimate=pl.CostEstimate(flops=40000000, bytes_accessed=1000000, transcendentals=0),
    )(*operands)


def weight_kernel(
    hidden_ref, gained_ref, rms_ref, shrink_ref, attn_ref, q_ref,
    resid_ref, out_ref, held_ref, tile_ref, sems,
):
    rms = to_column(rms_ref[...])
    shrink = to_column(shrink_ref[...])
    for c in range(CH_Q):
        at = slice(c * QLEN, (c + 1) * QLEN)
        held_ref[at, :] = (
            rms[at] * gained_ref[c : c + 1, :] - shrink[at] * hidden_ref[at, :]
        ).astype(BF16)
    blocks, block = tile_ref.shape[0], tile_ref.shape[1]
    copies = [pltpu.make_async_copy(held_ref, resid_ref, sems.at[blocks])]
    copies[0].start()
    for b in range(blocks):
        at = slice(b * block, (b + 1) * block)
        tile_ref[b] = dot(attn_ref[at, :], held_ref[...], 1, 0).astype(BF16)
        copy = pltpu.make_async_copy(tile_ref.at[b], out_ref.at[pl.ds(b * block, block)], sems.at[b])
        copy.start()
        copies.append(copy)
    for copy in copies:
        copy.wait()


def weight_grads(hidden, gained, rms, shrink, attn_turned, q_all):
    tokens, cols = hidden.shape
    rows = attn_turned.shape[0]
    blocks = 8
    vmem = pl.BlockSpec(memory_space=pltpu.VMEM)
    anywhere = pl.BlockSpec(memory_space=pl.ANY)
    return pl.pallas_call(
        weight_kernel,
        out_shape=(
            jax.ShapeDtypeStruct((tokens, cols), BF16),
            jax.ShapeDtypeStruct((rows, cols), BF16),
        ),
        in_specs=[vmem] * 6,
        out_specs=(anywhere, anywhere),
        scratch_shapes=[
            pltpu.VMEM((tokens, cols), BF16),
            pltpu.VMEM((blocks, rows // blocks, cols), BF16),
            pltpu.SemaphoreType.DMA((blocks + 1,)),
        ],
        compiler_params=pltpu.CompilerParams(vmem_limit_bytes=VMEM_LIMIT),
        cost_estimate=pl.CostEstimate(
            flops=1100000000, bytes_accessed=7000000, transcendentals=0
        ),
    )(hidden, gained, rms, shrink, attn_turned, q_all)


def pool_sum_kernel(code_ref, weight_ref, q_ref, pool_ref, out_ref, spread_ref):
    group = LANES // WIDE
    steps = code_ref.shape[0] // group

    def lined(values):
        wide = tiled(values, WIDE, group)
        down = lax.broadcasted_iota(jnp.int32, wide.shape, 0)
        along = lax.broadcasted_iota(jnp.int32, wide.shape, 1)
        kept = jnp.where(along // WIDE == down % group, wide, 0.0)
        return jnp.sum(kept.reshape(wide.shape[0] // group, group, LANES), axis=1)

    code = code_ref[...]
    pool_row = lined(lax.shift_right_logical(code, 7).astype(F32)).astype(jnp.int32)
    query = lined(jnp.bitwise_and(code, 127).astype(F32)).astype(jnp.int32)
    peer = lax.broadcasted_iota(jnp.int32, (steps, LANES), 1) // WIDE
    query = jnp.where(query > 0, peer * Q_GRP + query - 1, -1)
    w_q = lined(weight_ref[:, :WIDE])
    w_n = lined(weight_ref[:, WIDE:])
    down = lax.broadcasted_iota(jnp.int32, (POOL_GRP, LANES), 0)
    across = lax.broadcasted_iota(jnp.int32, (group * Q_GRP, LANES), 0)
    own = jnp.zeros((POOL_GRP, LANES), F32)
    for step in range(steps):
        at = slice(step, step + 1)
        hot = down == pool_row[at]
        parts = split(jnp.where(hot, w_q[at], 0.0))
        pick = jnp.where(across == query[at], 1.0, 0.0).astype(BF16)
        spread_ref[:, step * group * Q_GRP : (step + 1) * group * Q_GRP] = dot(
            jnp.concatenate(parts, axis=0), pick, 1, 1
        ).astype(BF16)
        own += jnp.where(hot, w_n[at], 0.0)
    own = jnp.sum(own, axis=1, keepdims=True)
    width = 256
    for first in range(0, out_ref.shape[1], width):
        at = slice(first, first + width)
        both = dot(spread_ref[...], q_ref[:, at], 1, 0)
        out_ref[:, at] = (
            both[:POOL_GRP] + both[POOL_GRP:] - own * pool_ref[:, at].astype(F32)
        ).astype(BF16)


def pool_sum(code, weights, q_all, pool):
    vmem = pl.BlockSpec(memory_space=pltpu.VMEM)
    return pl.pallas_call(
        pool_sum_kernel,
        out_shape=jax.ShapeDtypeStruct(pool.shape, BF16),
        in_specs=[vmem] * 4,
        out_specs=vmem,
        scratch_shapes=[pltpu.VMEM((2 * POOL_GRP, q_all.shape[0]), BF16)],
        compiler_params=pltpu.CompilerParams(vmem_limit_bytes=VMEM_LIMIT),
        cost_estimate=pl.CostEstimate(
            flops=2500000000, bytes_accessed=9000000, transcendentals=0
        ),
    )(code, weights, q_all, pool)


def per_device(q, pos, pool, neg_owner, neg_row, resid_in, attn_out, out_weight, norm_gain):
    owners = lax.axis_size("dp")
    cols = q.shape[1]
    tokens = resid_in.shape[0]

    q_all = lax.all_gather(q, "dp", tiled=True)

    code, slot, owner_turned, place_hot = request_tables(
        neg_owner.T * POOL_GRP + neg_row.T, owners
    )
    wanted = lax.all_to_all(code, "dp", split_axis=0, concat_axis=0, tiled=True)
    pool_tiles = pool.reshape(POOL_GRP, SUB, LANES)
    fetched = fetch_rows(wanted, pool_tiles).reshape(owners, SLOTS * SUB, LANES)
    replies = lax.all_to_all(fetched, "dp", split_axis=0, concat_axis=0, tiled=True)

    fetched, q, pos, resid_in, attn_out = lax.optimization_barrier(
        (fetched, q, pos, resid_in, attn_out)
    )
    attn_turned = attn_out.T
    hidden = resid_in.astype(F32) + dot(attn_out, out_weight, 1, 0)
    hid_hi, hid_lo = split(hidden)
    scaled = jnp.concatenate(split(hidden * norm_gain[None, :]), axis=0)
    both = jnp.concatenate([pos, q], axis=0)
    scaled_dots = dot(jnp.concatenate([pos, q[:CH_Q]], axis=0), scaled, 1, 1)
    early = feature_total(
        jnp.concatenate(
            [
                scaled_dots[:, :tokens] + scaled_dots[:, tokens:],
                jnp.concatenate([dot(q, both, 1, 1), dot(pos, both, 1, 1)], axis=1),
                jnp.broadcast_to(jnp.sum(hidden * hidden, axis=1)[None, :], (8, tokens)),
            ],
            axis=0,
        )
    )
    hidden_back = feature_scatter(dot(hid_hi, out_weight, 1, 1) + dot(hid_lo, out_weight, 1, 1))
    eye = jnp.eye(Q_GRP, dtype=F32)
    scaled_pos = early[:Q_GRP]
    mine = jnp.arange(CH_Q)[:, None] == (jnp.arange(tokens) // QLEN)[None, :]
    scaled_q = jnp.sum(jnp.where(mine, early[Q_GRP : Q_GRP + CH_Q], 0.0), axis=0)[None, :]
    pairs = early[Q_GRP + CH_Q : 2 * Q_GRP + CH_Q]
    q_sq = jnp.sum(pairs[:, Q_GRP : 2 * Q_GRP] * eye, axis=0)
    p_sq = jnp.sum(pairs[:, 2 * Q_GRP : 3 * Q_GRP] * eye, axis=0)
    h_sq = early[2 * Q_GRP + CH_Q]
    inv_q = lax.rsqrt(q_sq + rep_epsilon)
    inv_p = lax.rsqrt(p_sq + rep_epsilon)
    inv_rms = lax.rsqrt(h_sq / D + norm_epsilon)
    s_in = pairs[:, :Q_GRP] * inv_q[:, None] * inv_p[None, :] * inv_temp
    exp_in = jnp.exp(s_in)
    sum_in = jnp.sum(exp_in, axis=1)[None, :]
    inv_q_row = inv_q[None, :]
    inv_p_row = inv_p[None, :]
    rms_row = inv_rms[None, :]
    (
        replies, sum_in, inv_q_row, inv_p_row, rms_row, scaled, scaled_pos, scaled_q,
        attn_turned, hidden_back, exp_in, s_in, hidden,
    ) = lax.optimization_barrier(
        (
            replies, sum_in, inv_q_row, inv_p_row, rms_row, scaled, scaled_pos,
            scaled_q, attn_turned, hidden_back, exp_in, s_in, hidden,
        )
    )

    sums, first_negs = row_sums(
        slot, replies.reshape(owners * SLOTS, SUB, LANES), q.reshape(Q_GRP, SUB, LANES)
    )
    first_negs = first_negs.reshape(NEG * CH_Q, cols)
    scaled_negs = dot(first_negs, scaled, 1, 1)
    scaled_negs = (scaled_negs[:, :tokens] + scaled_negs[:, tokens:]).reshape(NEG, CH_Q, tokens)
    scaled_negs = jnp.sum(jnp.where(mine[None], scaled_negs, 0.0), axis=1)
    late = feature_total(
        jnp.concatenate(
            [sums[:SUB], sums[SUB:], jnp.concatenate([scaled_negs, jnp.zeros((1, tokens), F32)])],
            axis=1,
        )
    )
    sent, coef_neg, s_neg, inv_n, denominator = soft(
        late, sum_in, inv_q_row, owner_turned, place_hot
    )
    got = lax.all_to_all(sent, "dp", split_axis=0, concat_axis=0, tiled=True)

    gained, halves, shrink, pos_grad = grads(
        late, coef_neg, s_neg, inv_n, denominator, exp_in, s_in, inv_q_row, inv_p_row, rms_row,
        scaled_pos, scaled_q, norm_gain[None, :], q, pos, first_negs,
    )
    gained_back = dot(halves, out_weight, 1, 1)
    gained_back = feature_scatter_small(gained_back[:CH_Q] + gained_back[CH_Q:])
    resid_grad, weight_grad = weight_grads(
        hidden, gained, rms_row, shrink, attn_turned, q_all
    )
    own = tokens // N_FS
    first = lax.axis_index("fsdp") * own
    own_rms = lax.dynamic_slice(rms_row[0], (first,), (own,))
    own_shrink = lax.dynamic_slice(shrink[0], (first,), (own,))
    gained_rows = jnp.broadcast_to(
        gained_back[:, None, :], (CH_Q // N_FS, QLEN, gained_back.shape[1])
    ).reshape(own, gained_back.shape[1])
    attn_grad = (own_rms[:, None] * gained_rows - own_shrink[:, None] * hidden_back).astype(BF16)
    resid_grad, got = lax.optimization_barrier((resid_grad, got))
    pool_grad = pool_sum(wanted, got, q_all, pool)
    return (
        resid_grad,
        attn_grad,
        weight_grad[None],
        pos_grad,
        pool_grad,
    )


def solution(mesh):
    placed = (
        P("dp", "fsdp"),
        P("dp", "fsdp"),
        P("dp", "fsdp"),
        P("dp", None),
        P("dp", None),
        P("dp", "fsdp"),
        P("dp", None),
        P(None, "fsdp"),
        P("fsdp"),
    )
    return jax.shard_map(
        per_device,
        mesh=mesh,
        in_specs=placed,
        out_specs=(
            P("dp", "fsdp"),
            P(("dp", "fsdp"), None),
            P("dp", None, "fsdp"),
            P("dp", "fsdp"),
            P("dp", "fsdp"),
        ),
        check_vma=False,
    )
```

```python
import jax
import jax.numpy as jnp
from jax import lax
from jax.experimental import pallas as pl
from jax.experimental.pallas import tpu as pltpu
from jax.sharding import PartitionSpec as P

D = 4096
NEG = 7
QLEN = 16
Q_GRP = 64
CH_Q = 16
POOL_GRP = 128
SLOTS = 14
WIDE = 16
SUB = 8
LANES = 128
VMEM_LIMIT = 24 * 1024 * 1024
N_FS = 4


inv_temp = 1.0 / 0.05
loss_scale = 32.0
rep_epsilon = 1e-06
norm_epsilon = 1e-05
F32 = jnp.float32
BF16 = jnp.bfloat16


def dot(a, b, ca, cb):
    return lax.dot_general(a, b, (((ca,), (cb,)), ((), ())), preferred_element_type=F32)


def dot_exact(a, b, ca, cb):
    return lax.dot_general(
        a, b, (((ca,), (cb,)), ((), ())), precision=lax.Precision.HIGHEST, preferred_element_type=F32
    )


def split(a):
    hi = a.astype(BF16)
    return hi, (a - hi.astype(F32)).astype(BF16)


def thirds(a):
    hi = a.astype(BF16)
    rest = a - hi.astype(F32)
    mid = rest.astype(BF16)
    return hi, mid, (rest - mid.astype(F32)).astype(BF16)


def shifted(value, step):
    return lax.ppermute(value, "fsdp", [(i, (i + step) % N_FS) for i in range(N_FS)])


def swapped(value, mask):
    return lax.ppermute(value, "fsdp", [(i, i ^ mask) for i in range(N_FS)])


def feature_total(rows):
    return rows + shifted(rows, 1) + shifted(rows, 3) + shifted(rows, 2)


def feature_scatter_small(rows):
    own = rows.shape[0] // N_FS
    me = lax.axis_index("fsdp")
    half = me // 2
    mine = lax.dynamic_slice(rows, (half * 2 * own, 0), (2 * own, rows.shape[1]))
    other = lax.dynamic_slice(rows, ((1 - half) * 2 * own, 0), (2 * own, rows.shape[1]))
    mine = mine + swapped(other, 3)
    side = me % 2
    kept = lax.dynamic_slice(mine, (side * own, 0), (own, rows.shape[1]))
    given = lax.dynamic_slice(mine, ((1 - side) * own, 0), (own, rows.shape[1]))
    return kept + swapped(given, 1)


def feature_scatter(rows):
    own = rows.shape[0] // N_FS
    me = lax.axis_index("fsdp")
    total = lax.dynamic_slice(rows, (me * own, 0), (own, rows.shape[1]))
    for step in (1, 3, 2):
        there = lax.rem(me + step, N_FS)
        part = lax.dynamic_slice(rows, (there * own, 0), (own, rows.shape[1]))
        total += shifted(part.astype(BF16), step).astype(F32)
    return total


def eye_of(rows, cols):
    down = lax.broadcasted_iota(jnp.int32, (rows, cols), 0)
    return (down == lax.broadcasted_iota(jnp.int32, (rows, cols), 1)).astype(F32)


def to_column(row):
    size = row.shape[1]
    return jnp.sum(eye_of(size, size) * row, axis=1, keepdims=True)


def tiled(values, period, times):
    width = period * times
    down = lax.broadcasted_iota(jnp.int32, (period, width), 0)
    along = lax.broadcasted_iota(jnp.int32, (period, width), 1)
    mask = (along % period == down).astype(F32).astype(BF16)
    return sum(dot(part, mask, 1, 0) for part in thirds(values))


def flat_row(values, times):
    rows, period = values.shape
    wide = tiled(values, period, times)
    down = lax.broadcasted_iota(jnp.int32, wide.shape, 0)
    along = lax.broadcasted_iota(jnp.int32, wide.shape, 1)
    return jnp.sum(jnp.where(along // period == down, wide, 0.0), axis=0, keepdims=True)


def request_kernel(name_ref, code_ref, slot_ref, turned_ref, place_ref):
    name = flat_row(name_ref[...].astype(F32), NEG).astype(jnp.int32)
    owner = lax.shift_right_logical(name, 7).astype(F32)
    row = jnp.bitwise_and(name, 127).astype(F32)
    requests = owner.shape[1]
    peers = turned_ref.shape[0]
    along = lax.broadcasted_iota(jnp.int32, (1, requests), 1)
    down = lax.broadcasted_iota(jnp.int32, (peers, requests), 0)
    hot = jnp.where(down == owner.astype(jnp.int32), 1.0, 0.0)
    turned = hot.astype(BF16)
    earlier = lax.broadcasted_iota(jnp.int32, (requests, requests), 0) < along
    before = dot(turned, jnp.where(earlier, 1.0, 0.0).astype(BF16), 1, 0)
    position = jnp.sum(hot * before, axis=0, keepdims=True)
    down = lax.broadcasted_iota(jnp.int32, (WIDE, requests), 0)
    place = jnp.where(down == position.astype(jnp.int32), 1.0, 0.0)
    query = (along % Q_GRP + 1).astype(F32)
    marks = jnp.concatenate([place * row, place * query], axis=0).astype(BF16)
    table = dot(turned, marks, 1, 1).astype(jnp.int32)
    code_ref[...] = table[:, :WIDE] * 128 + table[:, WIDE:]
    slot_ref[...] = (owner * SLOTS + position).astype(jnp.int32)
    turned_ref[...] = turned
    place_ref[...] = place.astype(BF16)


def request_tables(name, owners):
    requests = name.shape[0] * name.shape[1]
    vmem = pl.BlockSpec(memory_space=pltpu.VMEM)
    return pl.pallas_call(
        request_kernel,
        out_shape=(
            jax.ShapeDtypeStruct((owners, WIDE), jnp.int32),
            jax.ShapeDtypeStruct((1, requests), jnp.int32),
            jax.ShapeDtypeStruct((owners, requests), BF16),
            jax.ShapeDtypeStruct((WIDE, requests), BF16),
        ),
        in_specs=[vmem],
        out_specs=(vmem,) * 4,
        compiler_params=pltpu.CompilerParams(vmem_limit_bytes=VMEM_LIMIT),
        cost_estimate=pl.CostEstimate(flops=30000000, bytes_accessed=100000, transcendentals=0),
    )(name)


def fetch_kernel(code_ref, pool_ref, out_ref):
    @pl.loop(0, out_ref.shape[0], unroll=2)
    def _(peer):
        for place in range(SLOTS):
            out_ref[peer, place] = pool_ref[lax.shift_right_logical(code_ref[peer, place], 7)]


def fetch_rows(code, pool_tiles):
    peers = code.shape[0]
    return pl.pallas_call(
        fetch_kernel,
        out_shape=jax.ShapeDtypeStruct((peers, SLOTS, SUB, LANES), BF16),
        in_specs=[
            pl.BlockSpec(memory_space=pltpu.SMEM),
            pl.BlockSpec(memory_space=pltpu.VMEM),
        ],
        out_specs=pl.BlockSpec(memory_space=pltpu.VMEM),
        compiler_params=pltpu.CompilerParams(vmem_limit_bytes=VMEM_LIMIT),
        cost_estimate=pl.CostEstimate(flops=0, bytes_accessed=2 * 1835008, transcendentals=0),
    )(code, pool_tiles)


def row_sums_kernel(slot_ref, reply_ref, q_ref, sums_ref, first_ref, cos_ref, sq_ref):
    last = reply_ref.shape[0] - 1

    def one(query, keep):
        asked = q_ref[query].astype(F32)
        for k in range(NEG):
            row = reply_ref[jnp.clip(slot_ref[0, k * Q_GRP + query], 0, last)]
            if keep:
                first_ref[k * CH_Q + query] = row
            wide = row.astype(F32)
            at = pl.ds(k * Q_GRP + query, 1)
            cos_ref[at, :] = jnp.sum(wide * asked, axis=0, keepdims=True)
            sq_ref[at, :] = jnp.sum(wide * wide, axis=0, keepdims=True)

    pl.loop(0, CH_Q, unroll=2)(lambda query: one(query, True))
    pl.loop(CH_Q, Q_GRP, unroll=4)(lambda query: one(query, False))

    line = lax.broadcasted_iota(jnp.int32, (SUB, LANES), 0)
    for part, ref in ((0, cos_ref), (1, sq_ref)):
        total = jnp.zeros((SUB, Q_GRP), F32)
        for k in range(NEG):
            mask = (line == k).astype(F32).astype(BF16)
            for piece in thirds(ref[k * Q_GRP : (k + 1) * Q_GRP, :]):
                total += dot(mask, piece, 1, 1)
        sums_ref[part * SUB : (part + 1) * SUB, :] = total


def row_sums(slot, replies, q_tiles):
    return pl.pallas_call(
        row_sums_kernel,
        out_shape=(
            jax.ShapeDtypeStruct((2 * SUB, Q_GRP), F32),
            jax.ShapeDtypeStruct((NEG * CH_Q, SUB, LANES), BF16),
        ),
        in_specs=[
            pl.BlockSpec(memory_space=pltpu.SMEM),
            pl.BlockSpec(memory_space=pltpu.VMEM),
            pl.BlockSpec(memory_space=pltpu.VMEM),
        ],
        out_specs=(
            pl.BlockSpec(memory_space=pltpu.VMEM),
            pl.BlockSpec(memory_space=pltpu.VMEM),
        ),
        scratch_shapes=[
            pltpu.VMEM((NEG * Q_GRP, LANES), F32),
            pltpu.VMEM((NEG * Q_GRP, LANES), F32),
        ],
        compiler_params=pltpu.CompilerParams(vmem_limit_bytes=VMEM_LIMIT),
        cost_estimate=pl.CostEstimate(flops=2000000, bytes_accessed=2200000, transcendentals=0),
    )(slot, replies, q_tiles)


def soft_kernel(
    late_ref, sum_ref, inv_q_ref, owner_ref, place_ref, sent_ref, coef_ref, logit_ref, inv_n_ref, den_ref
):
    late = late_ref[...]
    inv_q = inv_q_ref[...]
    inv_n = lax.rsqrt(late[:, Q_GRP : 2 * Q_GRP] + rep_epsilon)
    logit = late[:, :Q_GRP] * inv_q * inv_n * inv_temp
    used = lax.broadcasted_iota(jnp.int32, logit.shape, 0) < NEG
    raised = jnp.where(used, jnp.exp(logit), 0.0)
    total = sum_ref[...] + jnp.sum(raised, axis=0, keepdims=True)
    coef = raised / total
    coef_ref[...] = coef
    logit_ref[...] = logit
    inv_n_ref[...] = inv_n
    den_ref[...] = total
    w_q = flat_row(loss_scale * inv_temp * coef * inv_q * inv_n, NEG)
    w_n = flat_row(loss_scale * coef * logit * inv_n * inv_n, NEG)
    owner = owner_ref[...].astype(F32)
    parts = split(owner * w_q) + split(owner * w_n)
    placed = dot(jnp.concatenate(parts, axis=0), place_ref[...], 1, 1)
    peers = owner.shape[0]
    sent_ref[:, :WIDE] = placed[:peers] + placed[peers : 2 * peers]
    sent_ref[:, WIDE:] = placed[2 * peers : 3 * peers] + placed[3 * peers :]


def soft(late, sum_in, inv_q, owner_turned, place_hot):
    small = jax.ShapeDtypeStruct((SUB, Q_GRP), F32)
    vmem = pl.BlockSpec(memory_space=pltpu.VMEM)
    return pl.pallas_call(
        soft_kernel,
        out_shape=(
            jax.ShapeDtypeStruct((owner_turned.shape[0], 2 * WIDE), F32),
            small,
            small,
            small,
            jax.ShapeDtypeStruct((1, Q_GRP), F32),
        ),
        in_specs=[vmem] * 5,
        out_specs=(vmem,) * 5,
        compiler_params=pltpu.CompilerParams(vmem_limit_bytes=VMEM_LIMIT),
        cost_estimate=pl.CostEstimate(flops=8000000, bytes_accessed=100000, transcendentals=512),
    )(late, sum_in, inv_q, owner_turned, place_hot)


def grads_kernel(
    late_ref, coef_ref, logit_ref, inv_n_ref, den_ref, exp_ref, s_ref, inv_q_ref, inv_p_ref,
    rms_ref, scaled_pos_ref, scaled_q_ref, gain_ref, q_ref, pos_ref, negs_ref,
    gained_ref, halves_ref, shrink_ref, pos_grad_ref,
):
    eye = eye_of(Q_GRP, Q_GRP)
    inv_q_row = inv_q_ref[...]
    inv_p_row = inv_p_ref[...]
    inv_q = to_column(inv_q_row)
    coef_neg = coef_ref[...]
    coef_in = exp_ref[...] / to_column(den_ref[...]) - eye
    product = coef_in * s_ref[...]
    neg_dot = jnp.sum(coef_neg * logit_ref[...], axis=0, keepdims=True)
    self_dot = loss_scale * (jnp.sum(product, axis=1, keepdims=True) + to_column(neg_dot))
    scale_dir = loss_scale * inv_temp / QLEN * inv_q
    scale_own = inv_q * inv_q * self_dot * (1.0 / QLEN)
    of_pos = (coef_in * inv_p_row * scale_dir)[:CH_Q]
    neg_part = (coef_neg * inv_n_ref[...] * (loss_scale * inv_temp / QLEN) * inv_q_row)[:, :CH_Q]
    neg_row = flat_row(neg_part, NEG)
    down = lax.broadcasted_iota(jnp.int32, (CH_Q, NEG * CH_Q), 0)
    along = lax.broadcasted_iota(jnp.int32, (CH_Q, NEG * CH_Q), 1)
    of_neg = jnp.where(along % CH_Q == down, neg_row, 0.0)
    of_own = -eye[:CH_Q, :CH_Q] * scale_own[:CH_Q]
    both = (
        dot(jnp.concatenate(split(of_pos), axis=0), pos_ref[...], 1, 0)
        + dot(jnp.concatenate(split(of_neg), axis=0), negs_ref[...], 1, 0)
        + dot(jnp.concatenate(split(of_own), axis=0), q_ref[:CH_Q, :], 1, 0)
    )
    gained = (both[:CH_Q] + both[CH_Q:]) * gain_ref[...]
    gained_ref[...] = gained
    high, low = split(gained)
    halves_ref[:CH_Q, :] = high
    halves_ref[CH_Q:, :] = low
    tokens = CH_Q * QLEN
    down = lax.broadcasted_iota(jnp.int32, (CH_Q, tokens), 0)
    mine = lax.broadcasted_iota(jnp.int32, (CH_Q, tokens), 1) // QLEN == down
    inner = dot_exact(of_pos, scaled_pos_ref[...], 1, 0) - scale_own[:CH_Q] * scaled_q_ref[...]
    inner = jnp.sum(jnp.where(mine, inner, 0.0), axis=0, keepdims=True)
    mask = mine.astype(F32).astype(BF16)
    spread = sum(dot(part, mask, 1, 0) for part in thirds(neg_part))
    inner += jnp.sum(spread * late_ref[:, 2 * Q_GRP :], axis=0, keepdims=True)
    rms = rms_ref[...]
    shrink_ref[...] = rms * rms * rms * inner * (1.0 / D)
    back = coef_in * inv_q * (inv_p_row * (loss_scale * inv_temp))
    turned = dot(jnp.concatenate(split(back), axis=1), q_ref[...], 0, 0)
    less = to_column(inv_p_row * inv_p_row * loss_scale * jnp.sum(product, axis=0, keepdims=True))
    pos_grad_ref[...] = (
        turned[:Q_GRP] + turned[Q_GRP:] - less * pos_ref[...].astype(F32)
    ).astype(BF16)


def grads(*operands):
    vmem = pl.BlockSpec(memory_space=pltpu.VMEM)
    cols = operands[-1].shape[1]
    return pl.pallas_call(
        grads_kernel,
        out_shape=(
            jax.ShapeDtypeStruct((CH_Q, cols), F32),
            jax.ShapeDtypeStruct((2 * CH_Q, cols), BF16),
            jax.ShapeDtypeStruct((1, CH_Q * QLEN), F32),
            jax.ShapeDtypeStruct((Q_GRP, cols), BF16),
        ),
        in_specs=[vmem] * len(operands),
        out_specs=(vmem,) * 4,
        compiler_params=pltpu.CompilerParams(vmem_limit_bytes=VMEM_LIMIT),
        cost_estimate=pl.CostEstimate(flops=40000000, bytes_accessed=1000000, transcendentals=0),
    )(*operands)


def weight_kernel(
    hidden_ref, gained_ref, rms_ref, shrink_ref, attn_ref, resid_ref, out_ref, held_ref, tile_ref, sems
):
    rms = to_column(rms_ref[...])
    shrink = to_column(shrink_ref[...])
    for c in range(CH_Q):
        at = slice(c * QLEN, (c + 1) * QLEN)
        held_ref[at, :] = (
            rms[at] * gained_ref[c : c + 1, :] - shrink[at] * hidden_ref[at, :]
        ).astype(BF16)
    blocks, block = tile_ref.shape[0], tile_ref.shape[1]
    copies = [pltpu.make_async_copy(held_ref, resid_ref, sems.at[blocks])]
    copies[0].start()
    for b in range(blocks):
        at = slice(b * block, (b + 1) * block)
        tile_ref[b] = dot(attn_ref[at, :], held_ref[...], 1, 0).astype(BF16)
        copy = pltpu.make_async_copy(tile_ref.at[b], out_ref.at[pl.ds(b * block, block)], sems.at[b])
        copy.start()
        copies.append(copy)
    for copy in copies:
        copy.wait()


def weight_grads(hidden, gained, rms, shrink, attn_turned):
    tokens, cols = hidden.shape
    rows = attn_turned.shape[0]
    blocks = 8
    vmem = pl.BlockSpec(memory_space=pltpu.VMEM)
    anywhere = pl.BlockSpec(memory_space=pl.ANY)
    return pl.pallas_call(
        weight_kernel,
        out_shape=(
            jax.ShapeDtypeStruct((tokens, cols), BF16),
            jax.ShapeDtypeStruct((rows, cols), BF16),
        ),
        in_specs=[vmem] * 5,
        out_specs=(anywhere, anywhere),
        scratch_shapes=[
            pltpu.VMEM((tokens, cols), BF16),
            pltpu.VMEM((blocks, rows // blocks, cols), BF16),
            pltpu.SemaphoreType.DMA((blocks + 1,)),
        ],
        compiler_params=pltpu.CompilerParams(vmem_limit_bytes=VMEM_LIMIT),
        cost_estimate=pl.CostEstimate(
            flops=1100000000, bytes_accessed=7000000, transcendentals=0
        ),
    )(hidden, gained, rms, shrink, attn_turned)


def pool_sum_kernel(code_ref, weight_ref, q_ref, pool_ref, out_ref, spread_ref):
    group = LANES // WIDE
    steps = code_ref.shape[0] // group

    def lined(values):
        wide = tiled(values, WIDE, group)
        down = lax.broadcasted_iota(jnp.int32, wide.shape, 0)
        along = lax.broadcasted_iota(jnp.int32, wide.shape, 1)
        kept = jnp.where(along // WIDE == down % group, wide, 0.0)
        return jnp.sum(kept.reshape(wide.shape[0] // group, group, LANES), axis=1)

    code = code_ref[...]
    pool_row = lined(lax.shift_right_logical(code, 7).astype(F32)).astype(jnp.int32)
    query = lined(jnp.bitwise_and(code, 127).astype(F32)).astype(jnp.int32)
    peer = lax.broadcasted_iota(jnp.int32, (steps, LANES), 1) // WIDE
    query = jnp.where(query > 0, peer * Q_GRP + query - 1, -1)
    w_q = lined(weight_ref[:, :WIDE])
    w_n = lined(weight_ref[:, WIDE:])
    down = lax.broadcasted_iota(jnp.int32, (POOL_GRP, LANES), 0)
    across = lax.broadcasted_iota(jnp.int32, (group * Q_GRP, LANES), 0)
    own = jnp.zeros((POOL_GRP, LANES), F32)
    for step in range(steps):
        at = slice(step, step + 1)
        hot = down == pool_row[at]
        parts = split(jnp.where(hot, w_q[at], 0.0))
        pick = jnp.where(across == query[at], 1.0, 0.0).astype(BF16)
        spread_ref[:, step * group * Q_GRP : (step + 1) * group * Q_GRP] = dot(
            jnp.concatenate(parts, axis=0), pick, 1, 1
        ).astype(BF16)
        own += jnp.where(hot, w_n[at], 0.0)
    own = jnp.sum(own, axis=1, keepdims=True)
    width = 256
    for first in range(0, out_ref.shape[1], width):
        at = slice(first, first + width)
        both = dot(spread_ref[...], q_ref[:, at], 1, 0)
        out_ref[:, at] = (
            both[:POOL_GRP] + both[POOL_GRP:] - own * pool_ref[:, at].astype(F32)
        ).astype(BF16)


def pool_sum(code, weights, q_all, pool):
    vmem = pl.BlockSpec(memory_space=pltpu.VMEM)
    return pl.pallas_call(
        pool_sum_kernel,
        out_shape=jax.ShapeDtypeStruct(pool.shape, BF16),
        in_specs=[vmem] * 4,
        out_specs=vmem,
        scratch_shapes=[pltpu.VMEM((2 * POOL_GRP, q_all.shape[0]), BF16)],
        compiler_params=pltpu.CompilerParams(vmem_limit_bytes=VMEM_LIMIT),
        cost_estimate=pl.CostEstimate(
            flops=2500000000, bytes_accessed=9000000, transcendentals=0
        ),
    )(code, weights, q_all, pool)


def per_device(q, pos, pool, neg_owner, neg_row, resid_in, attn_out, out_weight, norm_gain):
    owners = lax.axis_size("dp")
    cols = q.shape[1]
    tokens = resid_in.shape[0]

    q_all = lax.all_gather(q, "dp", tiled=True)

    code, slot, owner_turned, place_hot = request_tables(
        neg_owner.T * POOL_GRP + neg_row.T, owners
    )
    wanted = lax.all_to_all(code, "dp", split_axis=0, concat_axis=0, tiled=True)
    pool_tiles = pool.reshape(POOL_GRP, SUB, LANES)
    fetched = fetch_rows(wanted, pool_tiles).reshape(owners, SLOTS * SUB, LANES)
    replies = lax.all_to_all(fetched, "dp", split_axis=0, concat_axis=0, tiled=True)

    fetched, q, pos, resid_in, attn_out = lax.optimization_barrier(
        (fetched, q, pos, resid_in, attn_out)
    )
    attn_turned = attn_out.T
    hidden = resid_in.astype(F32) + dot(attn_out, out_weight, 1, 0)
    hid_hi, hid_lo = split(hidden)
    scaled = jnp.concatenate(split(hidden * norm_gain[None, :]), axis=0)
    both = jnp.concatenate([pos, q], axis=0)
    scaled_dots = dot(jnp.concatenate([pos, q[:CH_Q]], axis=0), scaled, 1, 1)
    early = feature_total(
        jnp.concatenate(
            [
                scaled_dots[:, :tokens] + scaled_dots[:, tokens:],
                jnp.concatenate([dot(q, both, 1, 1), dot(pos, both, 1, 1)], axis=1),
                jnp.broadcast_to(jnp.sum(hidden * hidden, axis=1)[None, :], (8, tokens)),
            ],
            axis=0,
        )
    )
    hidden_back = feature_scatter(dot(hid_hi, out_weight, 1, 1) + dot(hid_lo, out_weight, 1, 1))
    eye = jnp.eye(Q_GRP, dtype=F32)
    scaled_pos = early[:Q_GRP]
    mine = jnp.arange(CH_Q)[:, None] == (jnp.arange(tokens) // QLEN)[None, :]
    scaled_q = jnp.sum(jnp.where(mine, early[Q_GRP : Q_GRP + CH_Q], 0.0), axis=0)[None, :]
    pairs = early[Q_GRP + CH_Q : 2 * Q_GRP + CH_Q]
    q_sq = jnp.sum(pairs[:, Q_GRP : 2 * Q_GRP] * eye, axis=0)
    p_sq = jnp.sum(pairs[:, 2 * Q_GRP : 3 * Q_GRP] * eye, axis=0)
    h_sq = early[2 * Q_GRP + CH_Q]
    inv_q = lax.rsqrt(q_sq + rep_epsilon)
    inv_p = lax.rsqrt(p_sq + rep_epsilon)
    inv_rms = lax.rsqrt(h_sq / D + norm_epsilon)
    s_in = pairs[:, :Q_GRP] * inv_q[:, None] * inv_p[None, :] * inv_temp
    exp_in = jnp.exp(s_in)
    sum_in = jnp.sum(exp_in, axis=1)[None, :]
    inv_q_row = inv_q[None, :]
    inv_p_row = inv_p[None, :]
    rms_row = inv_rms[None, :]
    (
        replies, sum_in, inv_q_row, inv_p_row, rms_row, scaled, scaled_pos, scaled_q,
        attn_turned, hidden_back, exp_in, s_in, hidden,
    ) = lax.optimization_barrier(
        (
            replies, sum_in, inv_q_row, inv_p_row, rms_row, scaled, scaled_pos,
            scaled_q, attn_turned, hidden_back, exp_in, s_in, hidden,
        )
    )

    sums, first_negs = row_sums(
        slot, replies.reshape(owners * SLOTS, SUB, LANES), q.reshape(Q_GRP, SUB, LANES)
    )
    first_negs = first_negs.reshape(NEG * CH_Q, cols)
    scaled_negs = dot(first_negs, scaled, 1, 1)
    scaled_negs = (scaled_negs[:, :tokens] + scaled_negs[:, tokens:]).reshape(NEG, CH_Q, tokens)
    scaled_negs = jnp.sum(jnp.where(mine[None], scaled_negs, 0.0), axis=1)
    late = feature_total(
        jnp.concatenate(
            [sums[:SUB], sums[SUB:], jnp.concatenate([scaled_negs, jnp.zeros((1, tokens), F32)])],
            axis=1,
        )
    )
    sent, coef_neg, s_neg, inv_n, denominator = soft(
        late, sum_in, inv_q_row, owner_turned, place_hot
    )
    got = lax.all_to_all(sent, "dp", split_axis=0, concat_axis=0, tiled=True)

    gained, halves, shrink, pos_grad = grads(
        late, coef_neg, s_neg, inv_n, denominator, exp_in, s_in, inv_q_row, inv_p_row, rms_row,
        scaled_pos, scaled_q, norm_gain[None, :], q, pos, first_negs,
    )
    gained_back = dot(halves, out_weight, 1, 1)
    gained_back = feature_scatter_small(gained_back[:CH_Q] + gained_back[CH_Q:])
    resid_grad, weight_grad = weight_grads(hidden, gained, rms_row, shrink, attn_turned)
    own = tokens // N_FS
    first = lax.axis_index("fsdp") * own
    own_rms = lax.dynamic_slice(rms_row[0], (first,), (own,))
    own_shrink = lax.dynamic_slice(shrink[0], (first,), (own,))
    gained_rows = jnp.broadcast_to(
        gained_back[:, None, :], (CH_Q // N_FS, QLEN, gained_back.shape[1])
    ).reshape(own, gained_back.shape[1])
    attn_grad = (own_rms[:, None] * gained_rows - own_shrink[:, None] * hidden_back).astype(BF16)
    pool_grad = pool_sum(wanted, got, q_all, pool)
    return (
        resid_grad,
        attn_grad,
        weight_grad[None],
        pos_grad,
        pool_grad,
    )


def solution(mesh):
    placed = (
        P("dp", "fsdp"),
        P("dp", "fsdp"),
        P("dp", "fsdp"),
        P("dp", None),
        P("dp", None),
        P("dp", "fsdp"),
        P("dp", None),
        P(None, "fsdp"),
        P("fsdp"),
    )
    return jax.shard_map(
        per_device,
        mesh=mesh,
        in_specs=placed,
        out_specs=(
            P("dp", "fsdp"),
            P(("dp", "fsdp"), None),
            P("dp", None, "fsdp"),
            P("dp", "fsdp"),
            P("dp", "fsdp"),
        ),
        check_vma=False,
    )
```
